32 devices in a mesh: seq: 8 (over z, y), mp: 4 (over x, core).
Axes of the slice: x: 2, y: 2, z: 4, core: 2. Of those that a mesh axis runs over, the one named last changes fastest.
Arguments:
- queries: bfloat16 [16384, 4096], P('seq', 'mp'), may hold values from -1000 to 1000, as said below
- encoded: bfloat16 [256, 32, 896], P('seq'), may hold values from -6 to 6
- w_kv: bfloat16 [896, 2, 4096], P(None, None, 'mp'), may hold values from -0.1875 to 0.1875
- retrieved: int32 [256, 2], P('seq'), may hold values from 0 to 255, as said below
Outputs:
- attended: bfloat16 [16384, 4096], P('seq', 'mp')
The draws below stay inside these ranges and needn't reach their ends.
Inputs may be any that keep to these rules, and one draw needn't show every extreme that they name: Decoder queries; their rows have unequal scales. `retrieved`: tile i is stored on index i // 32 of seq; of the 64 ids of one index of seq, exactly 8 name tiles stored on each index of seq; a tile may be named by many groups.
All inputs are finite; a program needn't handle non-finite values.
Results may differ from the reference program's by a relative error of at most 0.012.
Values may be sent and summed in bfloat16 or wider, within the bound.
No kernel may reach another device: no remote copies, remote signals or barrier semaphores. Data moves between devices by JAX's collectives and lax.ppermute only.
A program may use at most 128 MiB of HBM per device.

```python
import math
import jax
import jax.numpy as jnp
from jax import lax

D = 4096
HEADS = 32
D_ENC = 896
GROUP = 64
R = 32
CH_DEV = 32
HEAD_DIM = 128
GROUPS = 256
TOKENS = 16384
NB_DEV = 32
NBR = 256


def draw_queries(key, part):
    key_base, key_scale = jax.random.split(key, 2)
    base = jnp.clip(jax.random.normal(key_base, (TOKENS, D), jnp.float32), -6.0, 6.0)
    row_scale = jnp.exp(jax.random.uniform(key_scale, (TOKENS, 1), jnp.float32, 0.0, math.log(3.0)))
    return (base * row_scale).astype(jnp.bfloat16)


def draw_retrieved(key, part):
    devices = GROUPS // CH_DEV
    ref_count = 2 * CH_DEV
    key_order, key_first, key_second = jax.random.split(key, 3)
    ref_order = jax.vmap(lambda one_key: jax.random.permutation(one_key, ref_count))(jax.random.split(key_order, devices))
    owners = ref_order % devices
    first = jax.random.randint(key_first, (devices, ref_count), 0, NB_DEV)
    second = jax.random.randint(key_second, (devices, ref_count), 0, NB_DEV)
    local_ids = first * second // NB_DEV
    tile_ids = owners * NB_DEV + local_ids
    return tile_ids.reshape(GROUPS, 2).astype(jnp.int32)


def levels(rng, dims, pieces, smallest, top_value):
    factor_of, own = 1.0, jax.random.fold_in(rng, 6)
    for axis_at, shards_of in pieces:
        heights = jnp.exp(jax.random.uniform(jax.random.fold_in(own, axis_at), (shards_of,), jnp.float32, smallest / len(pieces), top_value / len(pieces)))
        factor_of = factor_of * jnp.repeat(heights, dims[axis_at] // shards_of).reshape([-1 if axis == axis_at else 1 for axis in range(len(dims))])
    return factor_of


def normal_values(own_key, dims, deviation, reach, shards=(), held_as=jnp.bfloat16):
    values = jax.random.normal(own_key, dims, jnp.float32) * deviation
    if len(shards) > 0:
        values = levels(own_key, dims, shards, -0.22, 0.18) * values
    return jnp.clip(values, min=-reach, max=reach).astype(held_as)


def setup_inputs(seed: int = 0) -> dict:
    key_of = jax.random.split(jax.random.key(seed), 5)
    queries = draw_queries(jax.random.fold_in(key_of[4], 71), 0)
    encoded = normal_values(key_of[1], (NBR, R, D_ENC), 1.0, 6.0, ((0, 8),))
    w_kv = normal_values(key_of[2], (D_ENC, 2, D), D_ENC ** -0.5, 0.1875, ((2, 4),))
    retrieved = draw_retrieved(jax.random.fold_in(key_of[4], 71), 0)
    return {"queries": queries, "encoded": encoded, "w_kv": w_kv, "retrieved": retrieved}


def reference(queries, encoded, w_kv, retrieved):
    blocks = GROUPS // CH_DEV
    weights = w_kv.reshape(D_ENC, 2 * D).astype(jnp.float32)

    def one_block(operands):
        query_rows, tile_ids = operands
        tiles = jnp.take(encoded, tile_ids.reshape(2 * CH_DEV).astype(jnp.int32), axis=0)
        flat = jnp.dot(tiles.reshape(2 * CH_DEV * R, D_ENC).astype(jnp.float32), weights, preferred_element_type=jnp.float32)
        paired = flat.astype(jnp.bfloat16).reshape(CH_DEV, 2 * R, 2, HEADS, HEAD_DIM).astype(jnp.float32)
        key_rows = paired[:, :, 0]
        value_rows = paired[:, :, 1]
        query_heads = query_rows.reshape(CH_DEV, GROUP, HEADS, HEAD_DIM).astype(jnp.float32)
        scores = jnp.einsum("cthe,cshe->chts", query_heads, key_rows) * (HEAD_DIM ** -0.5)
        top = jnp.max(scores, axis=-1, keepdims=True)
        expd = jnp.exp(scores - top)
        probs = (expd / jnp.sum(expd, axis=-1, keepdims=True)).astype(jnp.bfloat16)
        mixed = jnp.einsum("chts,cshe->cthe", probs.astype(jnp.float32), value_rows)
        return mixed.astype(jnp.bfloat16).reshape(CH_DEV * GROUP, D)

    outputs = lax.map(one_block, (queries.reshape(blocks, CH_DEV * GROUP, D), retrieved.reshape(blocks, CH_DEV, 2)))
    return outputs.reshape(TOKENS, D)
```

```python
import functools

import jax
import jax.numpy as jnp
from jax import lax
from jax.experimental import pallas as pl
from jax.experimental.pallas import tpu as pltpu
from jax.sharding import PartitionSpec as P

GROUP = 64
HEAD_DIM = 128
MIB = 1024 * 1024


def hits_of(ids_ref, table_ref, owner, tile_count, ref_count):
    def step(i, count):
        tile_id = ids_ref[lax.rem(i, 2), lax.div(i, 2)]
        table_ref[count] = lax.rem(tile_id, tile_count)
        return count + (lax.div(tile_id, tile_count) == owner).astype(jnp.int32)

    lax.fori_loop(0, ref_count, step, jnp.int32(0), unroll=8)


def pick_kernel(rows, split, capacity, ids_ref, stored_ref, out_ref, table_ref, sem):
    seq_at, mp_at = lax.axis_index("seq"), lax.axis_index("mp")
    tile_count = stored_ref.shape[0]
    hits_of(ids_ref, table_ref, seq_at, tile_count, 2 * ids_ref.shape[1])
    first = pl.multiple_of((mp_at // 2) * rows, rows) if split else 0
    copies = []
    for j in range(capacity):
        source = stored_ref.at[table_ref[j], pl.ds(first, rows), :]
        copies.append(pltpu.make_async_copy(source, out_ref.at[j], sem.at[j]))
        copies[-1].start()
    for copy in copies:
        copy.wait()


def pick(ids, stored, rows, capacity):
    split = rows < stored.shape[1]
    return pl.pallas_call(
        functools.partial(pick_kernel, rows, split, capacity),
        out_shape=jax.ShapeDtypeStruct((capacity, rows, stored.shape[2]), stored.dtype),
        in_specs=[pl.BlockSpec(memory_space=pltpu.SMEM), pl.BlockSpec(memory_space=pl.ANY)],
        out_specs=pl.BlockSpec(memory_space=pl.ANY),
        scratch_shapes=[pltpu.SMEM((2 * ids.shape[1] + 1,), jnp.int32), pltpu.SemaphoreType.DMA((capacity,))],
        name="pick",
    )(ids, stored)


def slots_kernel(tile_count, seq_count, capacity, ids_ref, slots_ref, rank_ref):
    seq_at, core = lax.axis_index("seq"), lax.rem(lax.axis_index("mp"), 2)
    for owner in range(seq_count):
        rank_ref[owner] = 0

    def step(i, carry):
        owner = lax.div(ids_ref[lax.rem(i, 2), lax.div(i, 2)], tile_count)
        rank = rank_ref[owner]
        rank_ref[owner] = rank + 1
        apart = owner ^ seq_at
        part, side = lax.div(apart, 2), lax.rem(apart, 2)
        side = jnp.where(part == 0, side, side ^ core)
        slots_ref[i] = (part * 2 + side) * capacity + rank
        return carry

    lax.fori_loop(0, 2 * ids_ref.shape[1], step, 0)


def slots_of(ids, tile_count, seq_count, capacity):
    return pl.pallas_call(
        functools.partial(slots_kernel, tile_count, seq_count, capacity),
        out_shape=jax.ShapeDtypeStruct((2 * ids.shape[1],), jnp.int32),
        in_specs=[pl.BlockSpec(memory_space=pltpu.SMEM)],
        out_specs=pl.BlockSpec(memory_space=pltpu.SMEM),
        scratch_shapes=[pltpu.SMEM((seq_count,), jnp.int32)],
        name="slots",
    )(ids)


def project_kernel(count, *refs):
    pieces, weights_ref, out_ref = refs[:count], refs[count], refs[-1]
    if count == 2:
        for side, piece in enumerate(pieces):
            tiles, rows, width = piece.shape
            flat = jnp.dot(piece[...].reshape(tiles * rows, width), weights_ref[...], preferred_element_type=jnp.float32)
            out_ref[pl.ds(side * tiles, tiles)] = flat.astype(jnp.bfloat16).reshape(tiles, rows, -1)
    else:
        for at, piece in enumerate(pieces):
            side, half = at // 2, at % 2
            tiles, rows, width = piece.shape
            flat = jnp.dot(piece[...].reshape(tiles * rows, width), weights_ref[...], preferred_element_type=jnp.float32)
            out_ref[pl.ds(side * tiles, tiles), pl.ds(half * rows, rows)] = flat.astype(jnp.bfloat16).reshape(tiles, rows, -1)


def project(pieces, weights, held, part, shape):
    count = len(pieces)
    width, columns = weights.shape
    step = min(columns, 512)
    tiles = 2 * pieces[0].shape[0]
    rows = shape[1]
    operands = [*pieces, weights]
    in_specs = [pl.BlockSpec(p.shape, lambda n: (0, 0, 0)) for p in pieces]
    in_specs.append(pl.BlockSpec((width, step), lambda n: (0, n)))
    aliases = {}
    if held is not None:
        operands.append(held)
        in_specs.append(pl.BlockSpec(memory_space=pl.ANY))
        aliases = {count + 1: 0}
    flops = 2 * tiles * rows * width * columns
    return pl.pallas_call(
        functools.partial(project_kernel, count),
        grid=(columns // step,),
        out_shape=jax.ShapeDtypeStruct(shape, jnp.bfloat16),
        in_specs=in_specs,
        out_specs=pl.BlockSpec((tiles, rows, step), lambda n: (part, 0, n)),
        input_output_aliases=aliases,
        compiler_params=pltpu.CompilerParams(vmem_limit_bytes=32 * MIB),
        cost_estimate=pl.CostEstimate(flops=flops, bytes_accessed=8 * MIB, transcendentals=0),
        name="project",
    )(*operands)


def attend_kernel(heads, slots_ref, queries_ref, first_ref, second_ref, out_ref):
    width = heads * HEAD_DIM
    scale = HEAD_DIM ** (-0.5)
    for h in range(heads):
        key_at, value_at = pl.ds(h * HEAD_DIM, HEAD_DIM), pl.ds(width + h * HEAD_DIM, HEAD_DIM)
        keys = jnp.concatenate([first_ref[0, :, key_at], second_ref[0, :, key_at]], axis=0)
        values = jnp.concatenate([first_ref[0, :, value_at], second_ref[0, :, value_at]], axis=0)
        scores = lax.dot_general(
            queries_ref[:, key_at], keys, (((1,), (1,)), ((), ())), preferred_element_type=jnp.float32
        )
        top = jnp.max(scores, axis=-1, keepdims=True)
        expd = jnp.exp((scores - top) * scale)
        probs = (expd / jnp.sum(expd, axis=-1, keepdims=True)).astype(jnp.bfloat16)
        mixed = jnp.dot(probs, values, preferred_element_type=jnp.float32)
        out_ref[:, key_at] = mixed.astype(jnp.bfloat16)


def attend(queries, held, slots, heads):
    groups = queries.shape[0] // GROUP
    tile = (1, held.shape[1], held.shape[2])
    block = (GROUP, queries.shape[1])
    return pl.pallas_call(
        functools.partial(attend_kernel, heads),
        out_shape=jax.ShapeDtypeStruct(queries.shape, jnp.bfloat16),
        grid_spec=pltpu.PrefetchScalarGridSpec(
            num_scalar_prefetch=1,
            grid=(groups,),
            in_specs=[
                pl.BlockSpec(block, lambda c, s: (c, 0)),
                pl.BlockSpec(tile, lambda c, s: (s[2 * c], 0, 0)),
                pl.BlockSpec(tile, lambda c, s: (s[2 * c + 1], 0, 0)),
            ],
            out_specs=pl.BlockSpec(block, lambda c, s: (c, 0)),
        ),
        compiler_params=pltpu.CompilerParams(vmem_limit_bytes=32 * MIB),
        cost_estimate=pl.CostEstimate(flops=10**9, bytes_accessed=16 * MIB, transcendentals=10**6),
        name="attend",
    )(slots, queries, held, held)


def ref_ranks(owners):
    length = owners.shape[-1]
    position = jnp.arange(length)
    earlier = position[None, :] < position[:, None]
    same_owner = owners[..., :, None] == owners[..., None, :]
    return jnp.sum(same_owner & earlier, axis=-1)


def plain_body(queries, encoded, w_kv, retrieved):
    seq_count = lax.axis_size("seq")
    ref_count = 2 * retrieved.shape[0]
    tile_count = encoded.shape[0]
    capacity = (ref_count + seq_count - 1) // seq_count
    tile_ids = retrieved.reshape(ref_count)
    owners = tile_ids // tile_count
    slot_ids = owners * capacity + ref_ranks(owners)
    wanted = jnp.arange(seq_count * capacity, dtype=jnp.int32)[:, None] == slot_ids[None, :]
    request = jnp.sum(jnp.where(wanted, (tile_ids % tile_count)[None, :], 0), axis=1)
    asked = lax.all_to_all(request, "seq", split_axis=0, concat_axis=0, tiled=True)
    outgoing = jnp.take(encoded, asked, axis=0, mode="clip")
    tiles = lax.all_to_all(outgoing, "seq", split_axis=0, concat_axis=0, tiled=True)
    weights = w_kv.reshape(w_kv.shape[0], -1)
    flat = jnp.dot(tiles.reshape(-1, tiles.shape[2]), weights, preferred_element_type=jnp.float32)
    held = flat.astype(jnp.bfloat16).reshape(tiles.shape[0], tiles.shape[1], -1)
    return attend(queries, held, slot_ids, queries.shape[1] // HEAD_DIM)


def split_body(queries, encoded, w_kv, retrieved):
    seq_count, mp_count = lax.axis_size("seq"), lax.axis_size("mp")
    ref_count = 2 * retrieved.shape[0]
    tile_count, rows, width = encoded.shape
    capacity = ref_count // seq_count
    parts = seq_count // 2
    both = ("seq", "mp")

    def joint(move):
        return [(s * mp_count + m, move(s, m)) for s in range(seq_count) for m in range(mp_count)]

    def across(value, part):
        if part == 0:
            return lax.ppermute(value, "seq", [(s, s ^ 1) for s in range(seq_count)])
        return lax.ppermute(value, both, joint(lambda s, m: (s ^ (2 * part) ^ (m % 2)) * mp_count + m))

    def over_mp(value, flip):
        return lax.ppermute(value, "mp", [(m, m ^ flip) for m in range(mp_count)])

    ids = retrieved.T
    order = [p for p in range(parts - 1, 0, -1)] + [0]
    order = sorted(range(parts), key=lambda p: (-(p // 2), p))
    weights = w_kv.reshape(width, -1)
    slots = slots_of(ids, tile_count, seq_count, capacity)
    asked = {p: across(ids, p) for p in order}
    sent = {p: across(pick(asked[p], encoded, rows if p == 0 else rows // 2, capacity), p) for p in order}
    shape = (ref_count, rows, weights.shape[1])
    own = pick(ids, encoded, rows, capacity)
    held = None
    for p in [0, 1] + [q for q in order if q > 1]:
        if p == 0:
            pieces = [own, sent[p]]
        else:
            mine = sent[p]
            theirs = over_mp(mine, 2)
            pieces = [mine, theirs, over_mp(mine, 1), over_mp(theirs, 1)]
        held = project(pieces, weights, held, p, shape)
    return attend(queries, held, slots, queries.shape[1] // HEAD_DIM)


def body(queries, encoded, w_kv, retrieved):
    seq_count, mp_count = lax.axis_size("seq"), lax.axis_size("mp")
    ref_count = 2 * retrieved.shape[0]
    few = seq_count in (2, 4, 8) and mp_count == 4
    even = ref_count % seq_count == 0 and encoded.shape[1] % 32 == 0
    if few and even:
        return split_body(queries, encoded, w_kv, retrieved)
    return plain_body(queries, encoded, w_kv, retrieved)


def solution(mesh):
    in_specs = (P("seq", "mp"), P("seq", None, None), P(None, None, "mp"), P("seq", None))
    out_specs = P("seq", "mp")
    return jax.shard_map(body, mesh=mesh, in_specs=in_specs, out_specs=out_specs, check_vma=False)
```

```python
import functools

import jax
import jax.numpy as jnp
from jax import lax
from jax.experimental import pallas as pl
from jax.experimental.pallas import tpu as pltpu
from jax.sharding import PartitionSpec as P

GROUP = 64
HEAD_DIM = 128
MIB = 1024 * 1024


def pick_kernel(rows, split, capacity, ids_ref, stored_ref, out_ref, ids_at, table_ref, ids_sem, sem):
    tile_count = stored_ref.shape[0]
    fetch = pltpu.make_async_copy(ids_ref, ids_at, ids_sem)
    fetch.start()
    lowest = lax.axis_index("seq") * tile_count
    first = pl.multiple_of(lax.axis_index("mp") // 2 * rows, rows) if split else 0
    fetch.wait()
    count = jnp.int32(0)
    for k in range(ids_ref.shape[0]):
        for c in range(ids_ref.shape[1]):
            local = ids_at[k, c] - lowest
            table_ref[count] = local
            count += ((local >= 0) & (local < tile_count)).astype(jnp.int32)
    copies = []
    for j in range(capacity):
        local = jnp.clip(table_ref[j], 0, tile_count - 1)
        source = stored_ref.at[local, pl.ds(first, rows), :]
        copies.append(pltpu.make_async_copy(source, out_ref.at[j], sem.at[j]))
        copies[-1].start()
    for copy in copies:
        copy.wait()


def pick(ids, stored, rows, capacity):
    split = rows < stored.shape[1]
    return pl.pallas_call(
        functools.partial(pick_kernel, rows, split, capacity),
        out_shape=jax.ShapeDtypeStruct((capacity, rows, stored.shape[2]), stored.dtype),
        in_specs=[pl.BlockSpec(memory_space=pl.ANY), pl.BlockSpec(memory_space=pl.ANY)],
        out_specs=pl.BlockSpec(memory_space=pltpu.VMEM),
        scratch_shapes=[
            pltpu.SMEM(ids.shape, jnp.int32),
            pltpu.SMEM((ids.size + 1,), jnp.int32),
            pltpu.SemaphoreType.DMA,
            pltpu.SemaphoreType.DMA((capacity,)),
        ],
        name="pick",
    )(ids, stored)


def slots_kernel(tile_count, seq_count, capacity, ids_ref, slots_ref, rank_ref):
    seq_at, core = lax.axis_index("seq"), lax.rem(lax.axis_index("mp"), 2)
    for owner in range(seq_count):
        rank_ref[owner] = 0

    for k in range(ids_ref.shape[0]):
        for c in range(ids_ref.shape[1]):
            owner = lax.div(ids_ref[k, c], tile_count)
            rank = rank_ref[owner]
            rank_ref[owner] = rank + 1
            apart = owner ^ seq_at
            part, side = lax.div(apart, 2), lax.rem(apart, 2)
            side = jnp.where(part == 0, side, side ^ core)
            slots_ref[2 * c + k] = (part * 2 + side) * capacity + rank


def slots_of(ids, tile_count, seq_count, capacity):
    return pl.pallas_call(
        functools.partial(slots_kernel, tile_count, seq_count, capacity),
        out_shape=jax.ShapeDtypeStruct((2 * ids.shape[1],), jnp.int32),
        in_specs=[pl.BlockSpec(memory_space=pltpu.SMEM)],
        out_specs=pl.BlockSpec(memory_space=pltpu.SMEM),
        scratch_shapes=[pltpu.SMEM((seq_count,), jnp.int32)],
        name="slots",
    )(ids)


def project_kernel(count, *refs):
    pieces, weights_ref, out_ref = refs[:count], refs[count], refs[-1]
    if count == 2:
        for side, piece in enumerate(pieces):
            tiles, rows, width = piece.shape
            flat = jnp.dot(piece[...].reshape(tiles * rows, width), weights_ref[...], preferred_element_type=jnp.float32)
            out_ref[pl.ds(side * tiles, tiles)] = flat.astype(jnp.bfloat16).reshape(tiles, rows, -1)
    else:
        for at, piece in enumerate(pieces):
            side, half = at // 2, at % 2
            tiles, rows, width = piece.shape
            flat = jnp.dot(piece[...].reshape(tiles * rows, width), weights_ref[...], preferred_element_type=jnp.float32)
            out_ref[pl.ds(side * tiles, tiles), pl.ds(half * rows, rows)] = flat.astype(jnp.bfloat16).reshape(tiles, rows, -1)


def project(pieces, weights, held, part, shape):
    count = len(pieces)
    width, columns = weights.shape
    step = min(columns, 512)
    tiles = 2 * pieces[0].shape[0]
    rows = shape[1]
    operands = [*pieces, weights]
    in_specs = [pl.BlockSpec(p.shape, lambda n: (0, 0, 0)) for p in pieces]
    in_specs.append(pl.BlockSpec((width, step), lambda n: (0, n)))
    aliases = {}
    if held is not None:
        operands.append(held)
        in_specs.append(pl.BlockSpec(memory_space=pl.ANY))
        aliases = {count + 1: 0}
    flops = 2 * tiles * rows * width * columns
    return pl.pallas_call(
        functools.partial(project_kernel, count),
        grid=(columns // step,),
        out_shape=jax.ShapeDtypeStruct(shape, jnp.bfloat16),
        in_specs=in_specs,
        out_specs=pl.BlockSpec((tiles, rows, step), lambda n: (part, 0, n)),
        input_output_aliases=aliases,
        compiler_params=pltpu.CompilerParams(vmem_limit_bytes=32 * MIB),
        cost_estimate=pl.CostEstimate(flops=flops, bytes_accessed=8 * MIB, transcendentals=0),
        name="project",
    )(*operands)


def scores_of(queries, keys):
    both = lax.dot_general(
        jnp.concatenate(keys, axis=0),
        jnp.concatenate(queries, axis=0),
        (((1,), (1,)), ((), ())),
        preferred_element_type=jnp.float32,
    )
    rows = both.shape[0] // 2
    left = lax.broadcasted_iota(jnp.int32, (rows, both.shape[1]), 1) < both.shape[1] // 2
    return jnp.where(left, both[:rows], both[rows:])


def probs_of(scores):
    expd = jnp.exp((scores - jnp.max(scores, axis=0, keepdims=True)) * HEAD_DIM ** (-0.5))
    return (expd * (1.0 / jnp.sum(expd, axis=0, keepdims=True))).astype(jnp.bfloat16)


def mix(probs, values):
    both = lax.dot_general(
        probs, jnp.concatenate(values, axis=1), (((0,), (0,)), ((), ())), preferred_element_type=jnp.float32
    )
    half = both.shape[0] // 2
    return both[:half, :HEAD_DIM], both[half:, HEAD_DIM:]


def attend_kernel(heads, many, slots_ref, queries_ref, held_ref, out_ref):
    apart = 6
    first = pl.program_id(0) * many
    items = [(g, h) for g in range(many) for h in range(0, heads, 2)]

    def part_of(g, h):
        one, two = slots_ref[2 * (first + g)], slots_ref[2 * (first + g) + 1]
        at = pl.ds(h * HEAD_DIM, HEAD_DIM)
        return jnp.concatenate([held_ref[one, :, at], held_ref[two, :, at]], axis=0)

    scores, probs = {}, {}
    for now in range(len(items) + 2 * apart):
        if now < len(items):
            g, h = items[now]
            queries = [queries_ref[pl.ds(g * GROUP, GROUP), pl.ds((h + i) * HEAD_DIM, HEAD_DIM)] for i in range(2)]
            scores[now] = scores_of(queries, [part_of(g, h + i) for i in range(2)])
        if apart <= now < len(items) + apart:
            probs[now - apart] = probs_of(scores.pop(now - apart))
        if 2 * apart <= now:
            g, h = items[now - 2 * apart]
            mixed = mix(probs.pop(now - 2 * apart), [part_of(g, heads + h + i) for i in range(2)])
            for i in range(2):
                out_ref[pl.ds(g * GROUP, GROUP), pl.ds((h + i) * HEAD_DIM, HEAD_DIM)] = mixed[i].astype(jnp.bfloat16)


def attend(queries, held, slots, heads):
    groups = queries.shape[0] // GROUP
    many = 8 if groups % 8 == 0 else 1
    block = (many * GROUP, queries.shape[1])
    return pl.pallas_call(
        functools.partial(attend_kernel, heads, many),
        out_shape=jax.ShapeDtypeStruct(queries.shape, jnp.bfloat16),
        grid_spec=pltpu.PrefetchScalarGridSpec(
            num_scalar_prefetch=1,
            grid=(groups // many,),
            in_specs=[
                pl.BlockSpec(block, lambda c, s: (c, 0)),
                pl.BlockSpec(held.shape, lambda c, s: (0, 0, 0), pipeline_mode=pl.Buffered(1)),
            ],
            out_specs=pl.BlockSpec(block, lambda c, s: (c, 0)),
        ),
        compiler_params=pltpu.CompilerParams(vmem_limit_bytes=40 * MIB),
        cost_estimate=pl.CostEstimate(flops=10**9, bytes_accessed=16 * MIB, transcendentals=10**6),
        name="attend",
    )(slots, queries, held)


def ref_ranks(owners):
    length = owners.shape[-1]
    position = jnp.arange(length)
    earlier = position[None, :] < position[:, None]
    same_owner = owners[..., :, None] == owners[..., None, :]
    return jnp.sum(same_owner & earlier, axis=-1)


def plain_body(queries, encoded, w_kv, retrieved):
    seq_count = lax.axis_size("seq")
    ref_count = 2 * retrieved.shape[0]
    tile_count = encoded.shape[0]
    capacity = (ref_count + seq_count - 1) // seq_count
    tile_ids = retrieved.reshape(ref_count)
    owners = tile_ids // tile_count
    slot_ids = owners * capacity + ref_ranks(owners)
    wanted = jnp.arange(seq_count * capacity, dtype=jnp.int32)[:, None] == slot_ids[None, :]
    request = jnp.sum(jnp.where(wanted, (tile_ids % tile_count)[None, :], 0), axis=1)
    asked = lax.all_to_all(request, "seq", split_axis=0, concat_axis=0, tiled=True)
    outgoing = jnp.take(encoded, asked, axis=0, mode="clip")
    tiles = lax.all_to_all(outgoing, "seq", split_axis=0, concat_axis=0, tiled=True)
    weights = w_kv.reshape(w_kv.shape[0], -1)
    flat = jnp.dot(tiles.reshape(-1, tiles.shape[2]), weights, preferred_element_type=jnp.float32)
    held = flat.astype(jnp.bfloat16).reshape(tiles.shape[0], tiles.shape[1], -1)
    return attend(queries, held, slot_ids, queries.shape[1] // HEAD_DIM)


def split_body(queries, encoded, w_kv, retrieved):
    seq_count, mp_count = lax.axis_size("seq"), lax.axis_size("mp")
    ref_count = 2 * retrieved.shape[0]
    tile_count, rows, width = encoded.shape
    capacity = ref_count // seq_count
    parts = seq_count // 2
    both = ("seq", "mp")

    def joint(move):
        return [(s * mp_count + m, move(s, m)) for s in range(seq_count) for m in range(mp_count)]

    def across(value, part):
        if part == 0:
            return lax.ppermute(value, "seq", [(s, s ^ 1) for s in range(seq_count)])
        return lax.ppermute(value, both, joint(lambda s, m: (s ^ (2 * part) ^ (m % 2)) * mp_count + m))

    def over_mp(value, flip):
        return lax.ppermute(value, "mp", [(m, m ^ flip) for m in range(mp_count)])

    ids = retrieved.T
    order = sorted(range(parts), key=lambda p: (-(p // 2), p))
    weights = w_kv.reshape(width, -1)
    slots = slots_of(ids, tile_count, seq_count, capacity)
    asked = {p: across(ids, p) for p in order}
    sent = {p: across(pick(asked[p], encoded, rows if p == 0 else rows // 2, capacity), p) for p in order}
    shape = (ref_count, rows, weights.shape[1])
    own = pick(ids, encoded, rows, capacity)
    held = None
    for p in [0, 1] + [q for q in order if q > 1]:
        if p == 0:
            pieces = [own, sent[p]]
        else:
            mine = sent[p]
            theirs = over_mp(mine, 2)
            pieces = [mine, theirs, over_mp(mine, 1), over_mp(theirs, 1)]
        held = project(pieces, weights, held, p, shape)
    return attend(queries, held, slots, queries.shape[1] // HEAD_DIM)


def body(queries, encoded, w_kv, retrieved):
    seq_count, mp_count = lax.axis_size("seq"), lax.axis_size("mp")
    ref_count = 2 * retrieved.shape[0]
    few = seq_count in (2, 4, 8) and mp_count == 4
    even = ref_count % seq_count == 0 and encoded.shape[1] % 32 == 0
    if few and even:
        return split_body(queries, encoded, w_kv, retrieved)
    return plain_body(queries, encoded, w_kv, retrieved)


def solution(mesh):
    in_specs = (P("seq", "mp"), P("seq", None, None), P(None, None, "mp"), P("seq", None))
    out_specs = P("seq", "mp")
    return jax.shard_map(body, mesh=mesh, in_specs=in_specs, out_specs=out_specs, check_vma=False)
```

```python
import functools

import jax
import jax.numpy as jnp
from jax import lax
from jax.experimental import pallas as pl
from jax.experimental.pallas import tpu as pltpu
from jax.sharding import PartitionSpec as P

GROUP = 64
HEAD_DIM = 128
MIB = 1024 * 1024
LIGHT = pl.CostEstimate(flops=1, bytes_accessed=1, transcendentals=0)


def in_vmem(value):
    return pltpu.with_memory_space_constraint(value, pltpu.VMEM)


def plan_kernel(capacity, tile_count, ids_ref, slots_ref):
    seq_at, core = lax.axis_index("seq"), lax.rem(lax.axis_index("mp"), 2)
    bits = tile_count.bit_length() - 1
    half = capacity // 2
    counts = jnp.int32(0)
    for k in range(ids_ref.shape[0]):
        for c in range(ids_ref.shape[1]):
            owner = lax.shift_right_logical(ids_ref[k, c], bits)
            shift = owner * 4
            rank = lax.shift_right_logical(counts, shift) & (capacity - 1)
            counts += jnp.int32(1) << shift
            apart = owner ^ seq_at
            near = ((apart & 1) * capacity) + (rank ^ ((apart & 1) * core * half))
            far = ((apart & -2) + ((apart & 1) ^ core)) * capacity + rank
            slots_ref[2 * c + k] = jnp.where(apart < 2, near, far)


def plan(ids, tile_count, capacity):
    smem = pl.BlockSpec(memory_space=pltpu.SMEM)
    return pl.pallas_call(
        functools.partial(plan_kernel, capacity, tile_count),
        out_shape=jax.ShapeDtypeStruct((ids.size,), jnp.int32),
        in_specs=[smem],
        out_specs=smem,
        cost_estimate=LIGHT,
        name="plan",
    )(ids)


def pick_kernel(plans, keep, *refs):
    count = len(plans)
    asked, stored_ref, pieces = refs[:count], refs[count], refs[count + 1 : -4]
    here_ref = refs[-5] if keep else stored_ref
    ids_at, table_ref, ids_sem, sem = refs[-4:]
    tile_count, rows, _ = stored_ref.shape
    fetches = [pltpu.make_async_copy(ref, ids_at.at[i], ids_sem.at[i]) for i, ref in enumerate(asked)]
    for fetch in fetches:
        fetch.start()
    if keep:
        load = pltpu.make_async_copy(stored_ref, here_ref, sem)
        load.start()
    lowest, mp_at = lax.axis_index("seq") * tile_count, lax.axis_index("mp")
    half = pl.multiple_of(mp_at // 2 * (rows // 2), rows // 2)
    for i in range(count):
        fetches[i].wait()
        found = jnp.int32(0)
        for k in range(ids_at.shape[1]):
            for c in range(ids_at.shape[2]):
                local = ids_at[i, k, c] - lowest
                table_ref[i, found] = local
                found += ((local >= 0) & (local < tile_count)).astype(jnp.int32)
    if keep:
        load.wait()
    at = 0
    for i, (kind, sizes) in enumerate(plans):
        rank = (mp_at % 2) * sizes[0] if kind == "tiles" else 0
        for size in sizes:
            for j in range(size):
                local = jnp.clip(table_ref[i, rank + j], 0, tile_count - 1)
                pieces[at][j] = here_ref[local, pl.ds(half, rows // 2), :] if kind == "rows" else here_ref[local]
            rank += size
            at += 1


def pick(asked, stored, plans, keep):
    _, rows, width = stored.shape
    vmem = pl.BlockSpec(memory_space=pltpu.VMEM)
    shapes = [(size, rows // 2 if kind == "rows" else rows, width) for kind, sizes in plans for size in sizes]
    shapes += [stored.shape] * keep
    ids = asked[0]
    return pl.pallas_call(
        functools.partial(pick_kernel, plans, keep),
        out_shape=[pltpu.VMEM(shape, stored.dtype) for shape in shapes],
        in_specs=[vmem] * len(asked) + [pl.BlockSpec(memory_space=pl.ANY) if keep else vmem],
        out_specs=[vmem] * len(shapes),
        scratch_shapes=[
            pltpu.SMEM((len(asked), *ids.shape), jnp.int32),
            pltpu.SMEM((len(asked), ids.size + 1), jnp.int32),
            pltpu.SemaphoreType.DMA((len(asked),)),
            pltpu.SemaphoreType.DMA,
        ],
        compiler_params=pltpu.CompilerParams(vmem_limit_bytes=(52 if keep else 16) * MIB),
        cost_estimate=LIGHT,
        name="pick",
    )(*[in_vmem(a) for a in asked], stored)


def pace_kernel(slots_ref, turn_ref):
    turn_ref[0] = slots_ref[0]


def pace(slots):
    smem = pl.BlockSpec(memory_space=pltpu.SMEM)
    return pl.pallas_call(
        pace_kernel,
        out_shape=jax.ShapeDtypeStruct((1,), jnp.int32),
        in_specs=[smem],
        out_specs=smem,
        cost_estimate=pl.CostEstimate(flops=3 * 10**9, bytes_accessed=0, transcendentals=0),
        name="pace",
    )(slots)


def project_kernel(places, *refs):
    pieces, weights_ref, out_ref = refs[: len(places)], refs[len(places)], refs[-1]
    flat = jnp.concatenate([piece[...].reshape(-1, piece.shape[2]) for piece in pieces], axis=0)
    step = min(512, weights_ref.shape[1])
    for at in range(0, weights_ref.shape[1], step):
        columns = pl.ds(at, step)
        made = jnp.dot(flat, weights_ref[:, columns], preferred_element_type=jnp.float32).astype(jnp.bfloat16)
        done = 0
        for (tile, row), piece in zip(places, pieces):
            tiles, rows, _ = piece.shape
            part = made[done : done + tiles * rows].reshape(tiles, rows, -1)
            out_ref[pl.ds(tile, tiles), pl.ds(row, rows), columns] = part
            done += tiles * rows


def project(pieces, weights, held, shape, weight):
    count = len(pieces)
    vmem = pl.BlockSpec(memory_space=pltpu.VMEM)
    operands = [in_vmem(p) for _, _, p in pieces] + [weights]
    aliases = {}
    if held is not None:
        operands.append(held)
        aliases = {count + 1: 0}
    many = sum(p.shape[0] * p.shape[1] for _, _, p in pieces)
    return pl.pallas_call(
        functools.partial(project_kernel, [(tile, row) for tile, row, _ in pieces]),
        out_shape=pltpu.VMEM(shape, jnp.bfloat16),
        in_specs=[vmem] * len(operands),
        out_specs=vmem,
        input_output_aliases=aliases,
        compiler_params=pltpu.CompilerParams(vmem_limit_bytes=16 * MIB),
        cost_estimate=pl.CostEstimate(flops=many * weights.size * weight // 4, bytes_accessed=0, transcendentals=0),
        name="project",
    )(*operands)


def scores_of(queries, keys):
    both = lax.dot_general(
        jnp.concatenate(keys, axis=0),
        jnp.concatenate(queries, axis=0),
        (((1,), (1,)), ((), ())),
        preferred_element_type=jnp.float32,
    )
    rows = both.shape[0] // 2
    left = lax.broadcasted_iota(jnp.int32, (rows, both.shape[1]), 1) < both.shape[1] // 2
    return jnp.where(left, both[:rows], both[rows:])


def probs_of(scores):
    expd = jnp.exp((scores - jnp.max(scores, axis=0, keepdims=True)) * HEAD_DIM ** (-0.5))
    return (expd * (1.0 / jnp.sum(expd, axis=0, keepdims=True))).astype(jnp.bfloat16)


def mix(probs, values):
    both = lax.dot_general(
        probs, jnp.concatenate(values, axis=1), (((0,), (0,)), ((), ())), preferred_element_type=jnp.float32
    )
    half = both.shape[0] // 2
    return both[:half, :HEAD_DIM], both[half:, HEAD_DIM:]


def attend_kernel(heads, many, slots_ref, queries_ref, held_ref, out_ref):
    apart = 6
    first = pl.program_id(0) * many
    items = [(g, h) for g in range(many) for h in range(0, heads, 2)]

    def part_of(g, h):
        one, two = slots_ref[2 * (first + g)], slots_ref[2 * (first + g) + 1]
        at = pl.ds(h * HEAD_DIM, HEAD_DIM)
        return jnp.concatenate([held_ref[one, :, at], held_ref[two, :, at]], axis=0)

    scores, probs = {}, {}
    for now in range(len(items) + 2 * apart):
        if now < len(items):
            g, h = items[now]
            queries = [queries_ref[pl.ds(g * GROUP, GROUP), pl.ds((h + i) * HEAD_DIM, HEAD_DIM)] for i in range(2)]
            scores[now] = scores_of(queries, [part_of(g, h + i) for i in range(2)])
        if apart <= now < len(items) + apart:
            probs[now - apart] = probs_of(scores.pop(now - apart))
        if 2 * apart <= now:
            g, h = items[now - 2 * apart]
            mixed = mix(probs.pop(now - 2 * apart), [part_of(g, heads + h + i) for i in range(2)])
            for i in range(2):
                out_ref[pl.ds(g * GROUP, GROUP), pl.ds((h + i) * HEAD_DIM, HEAD_DIM)] = mixed[i].astype(jnp.bfloat16)


def attend(queries, held, slots, heads):
    groups = queries.shape[0] // GROUP
    many = 8 if groups % 8 == 0 else 1
    block = (many * GROUP, queries.shape[1])
    return pl.pallas_call(
        functools.partial(attend_kernel, heads, many),
        out_shape=jax.ShapeDtypeStruct(queries.shape, jnp.bfloat16),
        grid_spec=pltpu.PrefetchScalarGridSpec(
            num_scalar_prefetch=1,
            grid=(groups // many,),
            in_specs=[
                pl.BlockSpec(block, lambda c, s: (c, 0)),
                pl.BlockSpec(memory_space=pltpu.VMEM),
            ],
            out_specs=pl.BlockSpec(block, lambda c, s: (c, 0)),
        ),
        compiler_params=pltpu.CompilerParams(vmem_limit_bytes=24 * MIB),
        cost_estimate=pl.CostEstimate(flops=10**9, bytes_accessed=16 * MIB, transcendentals=10**6),
        name="attend",
    )(slots, queries, in_vmem(held))


def ref_ranks(owners):
    length = owners.shape[-1]
    position = jnp.arange(length)
    earlier = position[None, :] < position[:, None]
    same_owner = owners[..., :, None] == owners[..., None, :]
    return jnp.sum(same_owner & earlier, axis=-1)


def plain_body(queries, encoded, w_kv, retrieved):
    seq_count = lax.axis_size("seq")
    ref_count = 2 * retrieved.shape[0]
    tile_count = encoded.shape[0]
    capacity = (ref_count + seq_count - 1) // seq_count
    tile_ids = retrieved.reshape(ref_count)
    owners = tile_ids // tile_count
    slot_ids = owners * capacity + ref_ranks(owners)
    wanted = jnp.arange(seq_count * capacity, dtype=jnp.int32)[:, None] == slot_ids[None, :]
    request = jnp.sum(jnp.where(wanted, (tile_ids % tile_count)[None, :], 0), axis=1)
    asked = lax.all_to_all(request, "seq", split_axis=0, concat_axis=0, tiled=True)
    outgoing = jnp.take(encoded, asked, axis=0, mode="clip")
    tiles = lax.all_to_all(outgoing, "seq", split_axis=0, concat_axis=0, tiled=True)
    weights = w_kv.reshape(w_kv.shape[0], -1)
    flat = jnp.dot(tiles.reshape(-1, tiles.shape[2]), weights, preferred_element_type=jnp.float32)
    held = flat.astype(jnp.bfloat16).reshape(tiles.shape[0], tiles.shape[1], -1)
    return attend(queries, held, slot_ids, queries.shape[1] // HEAD_DIM)


def split_body(queries, encoded, w_kv, retrieved):
    seq_count, mp_count = lax.axis_size("seq"), lax.axis_size("mp")
    ref_count = 2 * retrieved.shape[0]
    tile_count, rows, width = encoded.shape
    capacity = ref_count // seq_count
    both = ("seq", "mp")

    def joint(move):
        return [(s * mp_count + m, move(s, m)) for s in range(seq_count) for m in range(mp_count)]

    def across(value, part):
        if part == 0:
            return lax.ppermute(value, "seq", [(s, s ^ 1) for s in range(seq_count)])
        return lax.ppermute(value, both, joint(lambda s, m: (s ^ (2 * part) ^ (m % 2)) * mp_count + m))

    def over_mp(value, flip):
        return lax.ppermute(value, "mp", [(m, m ^ flip) for m in range(mp_count)])

    def after(value, *others):
        return lax.optimization_barrier((value, *others))[0]

    ids = retrieved.T
    size = capacity // 2

    def spread(mine, first):
        theirs = over_mp(mine, 2)
        return [
            (first, 0, mine),
            (first, rows // 2, theirs),
            (first + capacity, 0, over_mp(mine, 1)),
            (first + capacity, rows // 2, over_mp(theirs, 1)),
        ]

    asked = [across(ids, p) for p in (2, 1)]
    picked2, *picked1, stored = pick(asked, encoded, [("rows", [capacity]), ("all", [size, size])], True)
    got2, got1 = across(picked2, 2), across(picked1[0], 1)
    ids, w_kv = after(ids, picked2), after(w_kv, picked2)
    weights = in_vmem(w_kv.reshape(width, -1))
    slots = plan(ids, tile_count, capacity)
    asked = lax.optimization_barrier((across(ids, 3), across(ids, 0), weights, slots))[:2]
    picked3, beside, own = pick(
        [*asked, ids], stored, [("rows", [capacity]), ("tiles", [size]), ("all", [capacity])], False
    )
    picked3, picked1[1], beside, got2, got1 = lax.optimization_barrier((picked3, picked1[1], beside, got2, got1))
    got3 = across(picked3, 3)
    rest1 = across(picked1[1], 1)
    theirs2 = over_mp(got2, 2)
    beside = across(beside, 0)
    shape = (ref_count, rows, weights.shape[1])
    theirs3 = over_mp(got3, 2)
    turn = pace(after(slots, got3))
    got1, rest1, beside, got2, theirs2 = lax.optimization_barrier((got1, rest1, beside, got2, theirs2, turn))[:5]
    first = 4 * capacity
    part2 = [
        (first, 0, got2),
        (first, rows // 2, theirs2),
        (first + capacity, 0, over_mp(got2, 1)),
        (first + capacity, rows // 2, over_mp(theirs2, 1)),
    ]
    first = 2 * capacity
    part1 = [
        (first, 0, got1),
        (first + size, 0, rest1),
        (first + capacity, 0, over_mp(got1, 1)),
        (first + capacity + size, 0, over_mp(rest1, 1)),
    ]
    part0 = [(0, 0, own), (capacity, 0, beside), (capacity + size, 0, over_mp(beside, 1))]
    held = None
    for pieces in (part0, part2, part1):
        held = project(pieces, weights, held, shape, 1)
    theirs3 = after(theirs3, held)
    first = 6 * capacity
    part3 = [(first, 0, got3), (first + capacity, 0, over_mp(got3, 1))]
    rest3 = [(first, rows // 2, theirs3), (first + capacity, rows // 2, over_mp(theirs3, 1))]
    held = project(part3, weights, held, shape, 64)
    held = project(rest3, weights, held, shape, 8)
    return attend(queries, held, slots, queries.shape[1] // HEAD_DIM)


def body(queries, encoded, w_kv, retrieved):
    seq_count, mp_count = lax.axis_size("seq"), lax.axis_size("mp")
    ref_count = 2 * retrieved.shape[0]
    few = seq_count == 8 and mp_count == 4
    capacity, tile_count = ref_count // seq_count, encoded.shape[0]
    even = capacity * seq_count == ref_count and capacity == 8 and tile_count & (tile_count - 1) == 0
    if few and even and encoded.shape[1] % 32 == 0:
        return split_body(queries, encoded, w_kv, retrieved)
    return plain_body(queries, encoded, w_kv, retrieved)


def solution(mesh):
    in_specs = (P("seq", "mp"), P("seq", None, None), P(None, None, "mp"), P("seq", None))
    out_specs = P("seq", "mp")
    return jax.shard_map(body, mesh=mesh, in_specs=in_specs, out_specs=out_specs, check_vma=False)
```

```python
import functools

import jax
import jax.numpy as jnp
from jax import lax
from jax.experimental import pallas as pl
from jax.experimental.pallas import tpu as pltpu
from jax.sharding import PartitionSpec as P

GROUP = 64
HEAD_DIM = 128
MIB = 1024 * 1024
PACE = 2 * 10**9
LIGHT = pl.CostEstimate(flops=1, bytes_accessed=1, transcendentals=0)


def in_vmem(value):
    return pltpu.with_memory_space_constraint(value, pltpu.VMEM)


def plan_kernel(capacity, tile_count, ids_ref, slots_ref):
    seq_at, core = lax.axis_index("seq"), lax.rem(lax.axis_index("mp"), 2)
    bits = tile_count.bit_length() - 1
    half = capacity // 2
    counts = jnp.int32(0)
    for k in range(ids_ref.shape[0]):
        for c in range(ids_ref.shape[1]):
            owner = lax.shift_right_logical(ids_ref[k, c], bits)
            shift = owner * 4
            rank = lax.shift_right_logical(counts, shift) & (capacity - 1)
            counts += jnp.int32(1) << shift
            apart = owner ^ seq_at
            near = ((apart & 1) * capacity) + (rank ^ ((apart & 1) * core * half))
            far = ((apart & -2) + ((apart & 1) ^ core)) * capacity + rank
            slots_ref[2 * c + k] = jnp.where(apart < 2, near, far)


def plan(ids, tile_count, capacity):
    smem = pl.BlockSpec(memory_space=pltpu.SMEM)
    return pl.pallas_call(
        functools.partial(plan_kernel, capacity, tile_count),
        out_shape=jax.ShapeDtypeStruct((ids.size,), jnp.int32),
        in_specs=[smem],
        out_specs=smem,
        cost_estimate=LIGHT,
        name="plan",
    )(ids)


def pick_kernel(plans, *refs):
    count = len(plans)
    asked, stored_ref, pieces = refs[:count], refs[count], refs[count + 1 : -5]
    here_ref, ids_at, table_ref, ids_sem, sem = refs[-5:]
    tile_count, rows, _ = stored_ref.shape
    fetches = [pltpu.make_async_copy(ref, ids_at.at[i], ids_sem.at[i]) for i, ref in enumerate(asked)]
    for fetch in fetches:
        fetch.start()
    load = pltpu.make_async_copy(stored_ref, here_ref, sem)
    load.start()
    lowest, mp_at = lax.axis_index("seq") * tile_count, lax.axis_index("mp")
    half = pl.multiple_of(mp_at // 2 * (rows // 2), rows // 2)
    for i in range(count):
        fetches[i].wait()
        found = jnp.int32(0)
        for k in range(ids_at.shape[1]):
            for c in range(ids_at.shape[2]):
                local = ids_at[i, k, c] - lowest
                table_ref[i, found] = local
                found += ((local >= 0) & (local < tile_count)).astype(jnp.int32)
    load.wait()
    at = 0
    for i, (kind, sizes) in enumerate(plans):
        rank = (mp_at % 2) * sizes[0] if kind == "tiles" else 0
        for size in sizes:
            for j in range(size):
                local = jnp.clip(table_ref[i, rank + j], 0, tile_count - 1)
                pieces[at][j] = here_ref[local, pl.ds(half, rows // 2), :] if kind == "rows" else here_ref[local]
            rank += size
            at += 1


def pick(asked, own, stored, plans):
    _, rows, width = stored.shape
    vmem, anywhere = pl.BlockSpec(memory_space=pltpu.VMEM), pl.BlockSpec(memory_space=pl.ANY)
    shapes = [(size, rows // 2 if kind == "rows" else rows, width) for kind, sizes in plans for size in sizes]
    return pl.pallas_call(
        functools.partial(pick_kernel, plans),
        out_shape=[pltpu.VMEM(shape, stored.dtype) for shape in shapes],
        in_specs=[vmem] * len(asked) + [anywhere, anywhere],
        out_specs=[vmem] * len(shapes),
        scratch_shapes=[
            pltpu.VMEM(stored.shape, stored.dtype),
            pltpu.SMEM((len(plans), *own.shape), jnp.int32),
            pltpu.SMEM((len(plans), own.size + 1), jnp.int32),
            pltpu.SemaphoreType.DMA((len(plans),)),
            pltpu.SemaphoreType.DMA,
        ],
        compiler_params=pltpu.CompilerParams(vmem_limit_bytes=52 * MIB),
        cost_estimate=LIGHT,
        name="pick",
    )(*[in_vmem(a) for a in asked], own, stored)


def turn_kernel(*refs):
    pass


def turn(values, others, flops):
    vmem = pl.BlockSpec(memory_space=pltpu.VMEM)
    count = len(values)
    return pl.pallas_call(
        turn_kernel,
        out_shape=[pltpu.VMEM(v.shape, v.dtype) for v in values],
        in_specs=[vmem] * count + [pl.BlockSpec(memory_space=pl.ANY)] * len(others),
        out_specs=[vmem] * count,
        input_output_aliases={i: i for i in range(count)},
        compiler_params=pltpu.CompilerParams(vmem_limit_bytes=16 * MIB),
        cost_estimate=pl.CostEstimate(flops=flops, bytes_accessed=1, transcendentals=0),
        name="turn",
    )(*[in_vmem(v) for v in values], *others)


def project_kernel(places, *refs):
    pieces, weights_ref, out_ref = refs[: len(places)], refs[len(places)], refs[-1]
    flat = jnp.concatenate([piece[...].reshape(-1, piece.shape[2]) for piece in pieces], axis=0)
    step = min(512, weights_ref.shape[1])
    for at in range(0, weights_ref.shape[1], step):
        columns = pl.ds(at, step)
        made = jnp.dot(flat, weights_ref[:, columns], preferred_element_type=jnp.float32).astype(jnp.bfloat16)
        done = 0
        for (tile, row), piece in zip(places, pieces):
            tiles, rows, _ = piece.shape
            part = made[done : done + tiles * rows].reshape(tiles, rows, -1)
            out_ref[pl.ds(tile, tiles), pl.ds(row, rows), columns] = part
            done += tiles * rows


def project(pieces, weights, held, shape, weight):
    count = len(pieces)
    vmem = pl.BlockSpec(memory_space=pltpu.VMEM)
    operands = [in_vmem(p) for _, _, p in pieces] + [weights]
    aliases = {}
    if held is not None:
        operands.append(held)
        aliases = {count + 1: 0}
    many = sum(p.shape[0] * p.shape[1] for _, _, p in pieces)
    return pl.pallas_call(
        functools.partial(project_kernel, [(tile, row) for tile, row, _ in pieces]),
        out_shape=pltpu.VMEM(shape, jnp.bfloat16),
        in_specs=[vmem] * len(operands),
        out_specs=vmem,
        input_output_aliases=aliases,
        compiler_params=pltpu.CompilerParams(vmem_limit_bytes=16 * MIB),
        cost_estimate=pl.CostEstimate(flops=many * weights.size * weight // 4, bytes_accessed=0, transcendentals=0),
        name="project",
    )(*operands)


def scores_of(queries, keys):
    both = lax.dot_general(
        jnp.concatenate(keys, axis=0),
        jnp.concatenate(queries, axis=0),
        (((1,), (1,)), ((), ())),
        preferred_element_type=jnp.float32,
    )
    rows = both.shape[0] // 2
    left = lax.broadcasted_iota(jnp.int32, (rows, both.shape[1]), 1) < both.shape[1] // 2
    return jnp.where(left, both[:rows], both[rows:])


def probs_of(scores):
    expd = jnp.exp((scores - jnp.max(scores, axis=0, keepdims=True)) * HEAD_DIM ** (-0.5))
    return (expd * (1.0 / jnp.sum(expd, axis=0, keepdims=True))).astype(jnp.bfloat16)


def mix(probs, values):
    both = lax.dot_general(
        probs, jnp.concatenate(values, axis=1), (((0,), (0,)), ((), ())), preferred_element_type=jnp.float32
    )
    half = both.shape[0] // 2
    return both[:half, :HEAD_DIM], both[half:, HEAD_DIM:]


def attend_kernel(heads, many, slots_ref, queries_ref, held_ref, out_ref):
    apart = 6
    first = pl.program_id(0) * many
    items = [(g, h) for g in range(many) for h in range(0, heads, 2)]

    def part_of(g, h):
        one, two = slots_ref[2 * (first + g)], slots_ref[2 * (first + g) + 1]
        at = pl.ds(h * HEAD_DIM, HEAD_DIM)
        return jnp.concatenate([held_ref[one, :, at], held_ref[two, :, at]], axis=0)

    scores, probs = {}, {}
    for now in range(len(items) + 2 * apart):
        if now < len(items):
            g, h = items[now]
            queries = [queries_ref[pl.ds(g * GROUP, GROUP), pl.ds((h + i) * HEAD_DIM, HEAD_DIM)] for i in range(2)]
            scores[now] = scores_of(queries, [part_of(g, h + i) for i in range(2)])
        if apart <= now < len(items) + apart:
            probs[now - apart] = probs_of(scores.pop(now - apart))
        if 2 * apart <= now:
            g, h = items[now - 2 * apart]
            mixed = mix(probs.pop(now - 2 * apart), [part_of(g, heads + h + i) for i in range(2)])
            for i in range(2):
                out_ref[pl.ds(g * GROUP, GROUP), pl.ds((h + i) * HEAD_DIM, HEAD_DIM)] = mixed[i].astype(jnp.bfloat16)


def attend(queries, held, slots, heads):
    groups = queries.shape[0] // GROUP
    many = 8 if groups % 8 == 0 else 1
    block = (many * GROUP, queries.shape[1])
    return pl.pallas_call(
        functools.partial(attend_kernel, heads, many),
        out_shape=jax.ShapeDtypeStruct(queries.shape, jnp.bfloat16),
        grid_spec=pltpu.PrefetchScalarGridSpec(
            num_scalar_prefetch=1,
            grid=(groups // many,),
            in_specs=[
                pl.BlockSpec(block, lambda c, s: (c, 0)),
                pl.BlockSpec(memory_space=pltpu.VMEM),
            ],
            out_specs=pl.BlockSpec(block, lambda c, s: (c, 0)),
        ),
        compiler_params=pltpu.CompilerParams(vmem_limit_bytes=24 * MIB),
        cost_estimate=pl.CostEstimate(flops=10**9, bytes_accessed=16 * MIB, transcendentals=10**6),
        name="attend",
    )(slots, queries, in_vmem(held))


def ref_ranks(owners):
    length = owners.shape[-1]
    position = jnp.arange(length)
    earlier = position[None, :] < position[:, None]
    same_owner = owners[..., :, None] == owners[..., None, :]
    return jnp.sum(same_owner & earlier, axis=-1)


def plain_body(queries, encoded, w_kv, retrieved):
    seq_count = lax.axis_size("seq")
    ref_count = 2 * retrieved.shape[0]
    tile_count = encoded.shape[0]
    capacity = (ref_count + seq_count - 1) // seq_count
    tile_ids = retrieved.reshape(ref_count)
    owners = tile_ids // tile_count
    slot_ids = owners * capacity + ref_ranks(owners)
    wanted = jnp.arange(seq_count * capacity, dtype=jnp.int32)[:, None] == slot_ids[None, :]
    request = jnp.sum(jnp.where(wanted, (tile_ids % tile_count)[None, :], 0), axis=1)
    asked = lax.all_to_all(request, "seq", split_axis=0, concat_axis=0, tiled=True)
    outgoing = jnp.take(encoded, asked, axis=0, mode="clip")
    tiles = lax.all_to_all(outgoing, "seq", split_axis=0, concat_axis=0, tiled=True)
    weights = w_kv.reshape(w_kv.shape[0], -1)
    flat = jnp.dot(tiles.reshape(-1, tiles.shape[2]), weights, preferred_element_type=jnp.float32)
    held = flat.astype(jnp.bfloat16).reshape(tiles.shape[0], tiles.shape[1], -1)
    return attend(queries, held, slot_ids, queries.shape[1] // HEAD_DIM)


def split_body(queries, encoded, w_kv, retrieved):
    seq_count, mp_count = lax.axis_size("seq"), lax.axis_size("mp")
    ref_count = 2 * retrieved.shape[0]
    tile_count, rows, width = encoded.shape
    capacity = ref_count // seq_count
    both = ("seq", "mp")

    def joint(move):
        return [(s * mp_count + m, move(s, m)) for s in range(seq_count) for m in range(mp_count)]

    def across(value, part):
        if part == 0:
            return lax.ppermute(value, "seq", [(s, s ^ 1) for s in range(seq_count)])
        return lax.ppermute(value, both, joint(lambda s, m: (s ^ (2 * part) ^ (m % 2)) * mp_count + m))

    def over_mp(value, flip):
        return lax.ppermute(value, "mp", [(m, m ^ flip) for m in range(mp_count)])


    ids = retrieved.T
    size = capacity // 2

    def spread(mine, first):
        theirs = over_mp(mine, 2)
        return [
            (first, 0, mine),
            (first, rows // 2, theirs),
            (first + capacity, 0, over_mp(mine, 1)),
            (first + capacity, rows // 2, over_mp(theirs, 1)),
        ]

    asked = [across(ids, p) for p in (2, 3, 1, 0)]
    kinds = [("rows", [capacity]), ("rows", [capacity]), ("all", [size, size]), ("tiles", [size]), ("all", [capacity])]
    picked2, picked3, *picked1, beside, own = pick(asked, ids, encoded, kinds)
    got2, got1, beside = across(picked2, 2), across(picked1[0], 1), across(beside, 0)
    weights = in_vmem(w_kv.reshape(width, -1))
    slots = plan(ids, tile_count, capacity)
    shape = (ref_count, rows, weights.shape[1])

    def add(held, pieces, weight):
        return project(pieces, weights, held, shape, weight)

    def core(value, tile, row, cuts):
        step = value.shape[0] // cuts
        return [(tile + at, row, over_mp(value[at : at + step], 1)) for at in range(0, value.shape[0], step)]

    at1, at2, at3 = 2 * capacity, 4 * capacity, 6 * capacity
    held = add(None, [(0, 0, own)], 1)
    picked3 = turn([picked3], [got2, held, slots], PACE)[0]
    next1, beside, got1, got2 = turn([picked1[1], beside, got1, got2], [picked3], 1)
    got3, rest1, theirs2 = across(picked3, 3), across(next1, 1), over_mp(got2, 2)
    held = add(held, [(capacity, 0, beside), *core(beside, capacity + size, 0, 2)], 1)
    held = add(held, [(at2, 0, got2), *core(got2, at2 + capacity, 0, 2)], 1)
    held = add(held, [(at1, 0, got1), *core(got1, at1 + capacity, 0, 2)], 1)
    got3 = turn([got3], [held], PACE)[0]
    theirs3 = over_mp(got3, 2)
    theirs2 = turn([theirs2], [got3], 1)[0]
    rest1 = turn([rest1], [theirs2], 1)[0]
    held = add(held, [(at2, rows // 2, theirs2), *core(theirs2, at2 + capacity, rows // 2, 2)], 1)
    held = add(held, [(at1 + size, 0, rest1), *core(rest1, at1 + capacity + size, 0, 2)], 1)
    theirs3 = turn([theirs3], [held], 1)[0]
    held = add(held, [(at3, 0, got3), *core(got3, at3 + capacity, 0, 2)], 64)
    held = add(held, [(at3, rows // 2, theirs3), *core(theirs3, at3 + capacity, rows // 2, 1)], 64)
    return attend(queries, held, slots, queries.shape[1] // HEAD_DIM)


def body(queries, encoded, w_kv, retrieved):
    seq_count, mp_count = lax.axis_size("seq"), lax.axis_size("mp")
    ref_count = 2 * retrieved.shape[0]
    few = seq_count == 8 and mp_count == 4
    capacity, tile_count = ref_count // seq_count, encoded.shape[0]
    even = capacity * seq_count == ref_count and capacity == 8 and tile_count & (tile_count - 1) == 0
    if few and even and encoded.shape[1] % 32 == 0:
        return split_body(queries, encoded, w_kv, retrieved)
    return plain_body(queries, encoded, w_kv, retrieved)


def solution(mesh):
    in_specs = (P("seq", "mp"), P("seq", None, None), P(None, None, "mp"), P("seq", None))
    out_specs = P("seq", "mp")
    return jax.shard_map(body, mesh=mesh, in_specs=in_specs, out_specs=out_specs, check_vma=False)
```

```python
import functools

import jax
import jax.numpy as jnp
from jax import lax
from jax.experimental import pallas as pl
from jax.experimental.pallas import tpu as pltpu
from jax.sharding import PartitionSpec as P

GROUP = 64
HEAD_DIM = 128
MIB = 1024 * 1024
PACE = 2 * 10**9
LIGHT = pl.CostEstimate(flops=1, bytes_accessed=1, transcendentals=0)


def in_vmem(value):
    return pltpu.with_memory_space_constraint(value, pltpu.VMEM)


def plan_kernel(capacity, ids_ref, stored_ref, slots_ref, own_ref, table_ref):
    seq_at, core = lax.axis_index("seq"), lax.rem(lax.axis_index("mp"), 2)
    tile_count = stored_ref.shape[0]
    bits = tile_count.bit_length() - 1
    half = capacity // 2
    counts = jnp.int32(0)
    for k in range(ids_ref.shape[0]):
        for c in range(ids_ref.shape[1]):
            tile_id = ids_ref[k, c]
            owner = lax.shift_right_logical(tile_id, bits)
            shift = owner * 4
            rank = lax.shift_right_logical(counts, shift) & (capacity - 1)
            counts += jnp.int32(1) << shift
            apart = owner ^ seq_at
            table_ref[apart * capacity + rank] = tile_id & (tile_count - 1)
            near = ((apart & 1) * capacity) + (rank ^ ((apart & 1) * core * half))
            far = ((apart & -2) + ((apart & 1) ^ core)) * capacity + rank
            slots_ref[2 * c + k] = jnp.where(apart < 2, near, far)
    for j in range(capacity):
        own_ref[j] = stored_ref[table_ref[j]]


def plan(ids, stored, capacity):
    smem, vmem = pl.BlockSpec(memory_space=pltpu.SMEM), pl.BlockSpec(memory_space=pltpu.VMEM)
    return pl.pallas_call(
        functools.partial(plan_kernel, capacity),
        out_shape=[
            jax.ShapeDtypeStruct((ids.size,), jnp.int32),
            pltpu.VMEM((capacity, *stored.shape[1:]), stored.dtype),
        ],
        in_specs=[smem, vmem],
        out_specs=[smem, vmem],
        scratch_shapes=[pltpu.SMEM((ids.size,), jnp.int32)],
        compiler_params=pltpu.CompilerParams(vmem_limit_bytes=16 * MIB),
        cost_estimate=LIGHT,
        name="plan",
    )(ids, stored)


def pick_kernel(plans, *refs):
    count = len(plans)
    asked, stored_ref, pieces = refs[:count], refs[count], refs[count + 1 : -5]
    here_ref, ids_at, table_ref, ids_sem, sem = refs[-5:]
    tile_count, rows, _ = stored_ref.shape
    fetches = [pltpu.make_async_copy(ref, ids_at.at[i], ids_sem.at[i]) for i, ref in enumerate(asked)]
    for fetch in fetches:
        fetch.start()
    load = pltpu.make_async_copy(stored_ref, here_ref, sem)
    load.start()
    lowest, mp_at = lax.axis_index("seq") * tile_count, lax.axis_index("mp")
    half = pl.multiple_of(mp_at // 2 * (rows // 2), rows // 2)
    for i in range(count):
        fetches[i].wait()
        found = jnp.int32(0)
        for k in range(ids_at.shape[1]):
            for c in range(ids_at.shape[2]):
                local = ids_at[i, k, c] - lowest
                table_ref[i, found] = local
                found += ((local >= 0) & (local < tile_count)).astype(jnp.int32)
    load.wait()
    at = 0
    for i, (kind, sizes) in enumerate(plans):
        rank = (mp_at % 2) * sizes[0] if kind == "tiles" else 0
        for size in sizes:
            for j in range(size):
                local = jnp.clip(table_ref[i, rank + j], 0, tile_count - 1)
                pieces[at][j] = here_ref[local, pl.ds(half, rows // 2), :] if kind == "rows" else here_ref[local]
            rank += size
            at += 1


def pick(asked, stored, plans):
    _, rows, width = stored.shape
    vmem = pl.BlockSpec(memory_space=pltpu.VMEM)
    shapes = [(size, rows // 2 if kind == "rows" else rows, width) for kind, sizes in plans for size in sizes]
    return pl.pallas_call(
        functools.partial(pick_kernel, plans),
        out_shape=[pltpu.VMEM(shape, stored.dtype) for shape in [*shapes, stored.shape]],
        in_specs=[vmem] * len(asked) + [pl.BlockSpec(memory_space=pl.ANY)],
        out_specs=[vmem] * (len(shapes) + 1),
        scratch_shapes=[
            pltpu.SMEM((len(plans), *asked[0].shape), jnp.int32),
            pltpu.SMEM((len(plans), asked[0].size + 1), jnp.int32),
            pltpu.SemaphoreType.DMA((len(plans),)),
            pltpu.SemaphoreType.DMA,
        ],
        compiler_params=pltpu.CompilerParams(vmem_limit_bytes=52 * MIB),
        cost_estimate=LIGHT,
        name="pick",
    )(*[in_vmem(a) for a in asked], stored)


def turn_kernel(*refs):
    pass


def turn(values, others, flops):
    vmem = pl.BlockSpec(memory_space=pltpu.VMEM)
    count = len(values)
    return pl.pallas_call(
        turn_kernel,
        out_shape=[pltpu.VMEM(v.shape, v.dtype) for v in values],
        in_specs=[vmem] * count + [pl.BlockSpec(memory_space=pl.ANY)] * len(others),
        out_specs=[vmem] * count,
        input_output_aliases={i: i for i in range(count)},
        compiler_params=pltpu.CompilerParams(vmem_limit_bytes=16 * MIB),
        cost_estimate=pl.CostEstimate(flops=flops, bytes_accessed=1, transcendentals=0),
        name="turn",
    )(*[in_vmem(v) for v in values], *others)


def project_kernel(places, *refs):
    pieces, weights_ref, out_ref = refs[: len(places)], refs[len(places)], refs[-1]
    flat = jnp.concatenate([piece[...].reshape(-1, piece.shape[2]) for piece in pieces], axis=0)
    step = min(512, weights_ref.shape[1])
    for at in range(0, weights_ref.shape[1], step):
        columns = pl.ds(at, step)
        made = jnp.dot(flat, weights_ref[:, columns], preferred_element_type=jnp.float32).astype(jnp.bfloat16)
        done = 0
        for (tile, row), piece in zip(places, pieces):
            tiles, rows, _ = piece.shape
            part = made[done : done + tiles * rows].reshape(tiles, rows, -1)
            out_ref[pl.ds(tile, tiles), pl.ds(row, rows), columns] = part
            done += tiles * rows


def project(pieces, weights, held, shape, weight):
    count = len(pieces)
    vmem = pl.BlockSpec(memory_space=pltpu.VMEM)
    operands = [in_vmem(p) for _, _, p in pieces] + [weights]
    aliases = {}
    if held is not None:
        operands.append(held)
        aliases = {count + 1: 0}
    many = sum(p.shape[0] * p.shape[1] for _, _, p in pieces)
    return pl.pallas_call(
        functools.partial(project_kernel, [(tile, row) for tile, row, _ in pieces]),
        out_shape=pltpu.VMEM(shape, jnp.bfloat16),
        in_specs=[vmem] * len(operands),
        out_specs=vmem,
        input_output_aliases=aliases,
        compiler_params=pltpu.CompilerParams(vmem_limit_bytes=16 * MIB),
        cost_estimate=pl.CostEstimate(flops=many * weights.size * weight // 4, bytes_accessed=0, transcendentals=0),
        name="project",
    )(*operands)


def scores_of(queries, keys):
    both = lax.dot_general(
        jnp.concatenate(keys, axis=0),
        jnp.concatenate(queries, axis=0),
        (((1,), (1,)), ((), ())),
        preferred_element_type=jnp.float32,
    )
    rows = both.shape[0] // 2
    left = lax.broadcasted_iota(jnp.int32, (rows, both.shape[1]), 1) < both.shape[1] // 2
    return jnp.where(left, both[:rows], both[rows:])


def probs_of(scores):
    expd = jnp.exp((scores - jnp.max(scores, axis=0, keepdims=True)) * HEAD_DIM ** (-0.5))
    return (expd * (1.0 / jnp.sum(expd, axis=0, keepdims=True))).astype(jnp.bfloat16)


def mix(probs, values):
    both = lax.dot_general(
        probs, jnp.concatenate(values, axis=1), (((0,), (0,)), ((), ())), preferred_element_type=jnp.float32
    )
    half = both.shape[0] // 2
    return both[:half, :HEAD_DIM], both[half:, HEAD_DIM:]


def attend_kernel(heads, per, slots_ref, queries_ref, held_ref, out_ref, made_ref, sem):
    apart = 6
    groups = queries_ref.shape[0] // GROUP
    items = [(g, h) for g in range(groups) for h in range(0, heads, 2)]

    def part_of(g, h):
        one, two = slots_ref[2 * g], slots_ref[2 * g + 1]
        at = pl.ds(h * HEAD_DIM, HEAD_DIM)
        return jnp.concatenate([held_ref[one, :, at], held_ref[two, :, at]], axis=0)

    scores, probs, copies = {}, {}, []
    for now in range(len(items) + 2 * apart):
        if now < len(items):
            g, h = items[now]
            queries = [queries_ref[pl.ds(g * GROUP, GROUP), pl.ds((h + i) * HEAD_DIM, HEAD_DIM)] for i in range(2)]
            scores[now] = scores_of(queries, [part_of(g, h + i) for i in range(2)])
        if apart <= now < len(items) + apart:
            probs[now - apart] = probs_of(scores.pop(now - apart))
        if 2 * apart <= now:
            g, h = items[now - 2 * apart]
            mixed = mix(probs.pop(now - 2 * apart), [part_of(g, heads + h + i) for i in range(2)])
            for i in range(2):
                made_ref[pl.ds(g * GROUP, GROUP), pl.ds((h + i) * HEAD_DIM, HEAD_DIM)] = mixed[i].astype(jnp.bfloat16)
            if h == heads - 2 and g % per == per - 1:
                done = pl.ds((g + 1 - per) * GROUP, per * GROUP)
                copies.append(pltpu.make_async_copy(made_ref.at[done], out_ref.at[done], sem.at[g // per]))
                copies[-1].start()
    for copy in copies:
        copy.wait()


def attend(queries, held, slots, heads):
    groups = queries.shape[0] // GROUP
    per = 2 if groups % 2 == 0 else 1
    vmem = pl.BlockSpec(memory_space=pltpu.VMEM)
    return pl.pallas_call(
        functools.partial(attend_kernel, heads, per),
        out_shape=jax.ShapeDtypeStruct(queries.shape, jnp.bfloat16),
        in_specs=[pl.BlockSpec(memory_space=pltpu.SMEM), vmem, vmem],
        out_specs=pl.BlockSpec(memory_space=pl.ANY),
        scratch_shapes=[pltpu.VMEM(queries.shape, jnp.bfloat16), pltpu.SemaphoreType.DMA((groups // per,))],
        compiler_params=pltpu.CompilerParams(vmem_limit_bytes=24 * MIB),
        cost_estimate=pl.CostEstimate(flops=10**9, bytes_accessed=16 * MIB, transcendentals=10**6),
        name="attend",
    )(slots, in_vmem(queries), in_vmem(held))


def ref_ranks(owners):
    length = owners.shape[-1]
    position = jnp.arange(length)
    earlier = position[None, :] < position[:, None]
    same_owner = owners[..., :, None] == owners[..., None, :]
    return jnp.sum(same_owner & earlier, axis=-1)


def plain_body(queries, encoded, w_kv, retrieved):
    seq_count = lax.axis_size("seq")
    ref_count = 2 * retrieved.shape[0]
    tile_count = encoded.shape[0]
    capacity = (ref_count + seq_count - 1) // seq_count
    tile_ids = retrieved.reshape(ref_count)
    owners = tile_ids // tile_count
    slot_ids = owners * capacity + ref_ranks(owners)
    wanted = jnp.arange(seq_count * capacity, dtype=jnp.int32)[:, None] == slot_ids[None, :]
    request = jnp.sum(jnp.where(wanted, (tile_ids % tile_count)[None, :], 0), axis=1)
    asked = lax.all_to_all(request, "seq", split_axis=0, concat_axis=0, tiled=True)
    outgoing = jnp.take(encoded, asked, axis=0, mode="clip")
    tiles = lax.all_to_all(outgoing, "seq", split_axis=0, concat_axis=0, tiled=True)
    weights = w_kv.reshape(w_kv.shape[0], -1)
    flat = jnp.dot(tiles.reshape(-1, tiles.shape[2]), weights, preferred_element_type=jnp.float32)
    held = flat.astype(jnp.bfloat16).reshape(tiles.shape[0], tiles.shape[1], -1)
    return attend(queries, held, slot_ids, queries.shape[1] // HEAD_DIM)


def split_body(queries, encoded, w_kv, retrieved):
    seq_count, mp_count = lax.axis_size("seq"), lax.axis_size("mp")
    ref_count = 2 * retrieved.shape[0]
    tile_count, rows, width = encoded.shape
    capacity = ref_count // seq_count
    both = ("seq", "mp")

    def joint(move):
        return [(s * mp_count + m, move(s, m)) for s in range(seq_count) for m in range(mp_count)]

    def across(value, part):
        if part == 0:
            return lax.ppermute(value, "seq", [(s, s ^ 1) for s in range(seq_count)])
        return lax.ppermute(value, both, joint(lambda s, m: (s ^ (2 * part) ^ (m % 2)) * mp_count + m))

    def over_mp(value, flip):
        return lax.ppermute(value, "mp", [(m, m ^ flip) for m in range(mp_count)])


    ids = retrieved.T
    size, early = capacity // 2, capacity // 2

    def spread(mine, first):
        theirs = over_mp(mine, 2)
        return [
            (first, 0, mine),
            (first, rows // 2, theirs),
            (first + capacity, 0, over_mp(mine, 1)),
            (first + capacity, rows // 2, over_mp(theirs, 1)),
        ]

    asked = [across(ids, p) for p in (2, 3, 1, 0)]
    kinds = [("rows", [capacity]), ("rows", [capacity]), ("all", [early, capacity - early]), ("tiles", [size])]
    picked2, picked3, *picked1, beside, stored = pick(asked, encoded, kinds)
    got2, got1, beside = across(picked2, 2), across(picked1[0], 1), across(beside, 0)
    weights = in_vmem(w_kv.reshape(width, -1))
    slots, own = plan(ids, stored, capacity)
    shape = (ref_count, rows, weights.shape[1])

    def add(held, pieces, weight):
        return project(pieces, weights, held, shape, weight)

    def core(value, tile, row, cuts):
        step = value.shape[0] // cuts
        return [(tile + at, row, over_mp(value[at : at + step], 1)) for at in range(0, value.shape[0], step)]

    at1, at2, at3 = 2 * capacity, 4 * capacity, 6 * capacity
    held = add(None, [(0, 0, own)], 1)
    picked3 = turn([picked3], [got2, held, slots], PACE)[0]
    next1, beside, got1, got2 = turn([picked1[1], beside, got1, got2], [picked3], 1)
    got3, rest1, theirs2 = across(picked3, 3), across(next1, 1), over_mp(got2, 2)
    held = add(held, [(capacity, 0, beside), *core(beside, capacity + size, 0, 2)], 1)
    held = add(held, [(at2, 0, got2), *core(got2, at2 + capacity, 0, 2)], 1)
    held = add(held, [(at1, 0, got1), *core(got1, at1 + capacity, 0, 1 if early % 2 else 2)], 1)
    got3 = turn([got3], [held], PACE)[0]
    theirs3 = over_mp(got3, 2)
    queries = in_vmem(queries)
    theirs2 = turn([theirs2], [got3], 1)[0]
    rest1 = turn([rest1], [theirs2, queries], 1)[0]
    held = add(held, [(at2, rows // 2, theirs2), *core(theirs2, at2 + capacity, rows // 2, 2)], 1)
    held = add(held, [(at1 + early, 0, rest1), *core(rest1, at1 + capacity + early, 0, 1 if early % 2 or early > size else 2)], 1)
    theirs3 = turn([theirs3], [held], 1)[0]
    held = add(held, [(at3, 0, got3), *core(got3, at3 + capacity, 0, 1)], 64)
    held = add(held, [(at3, rows // 2, theirs3), *core(theirs3, at3 + capacity, rows // 2, 1)], 64)
    return attend(queries, held, slots, queries.shape[1] // HEAD_DIM)


def body(queries, encoded, w_kv, retrieved):
    seq_count, mp_count = lax.axis_size("seq"), lax.axis_size("mp")
    ref_count = 2 * retrieved.shape[0]
    few = seq_count == 8 and mp_count == 4
    capacity, tile_count = ref_count // seq_count, encoded.shape[0]
    even = capacity * seq_count == ref_count and capacity == 8 and tile_count & (tile_count - 1) == 0
    if few and even and encoded.shape[1] % 32 == 0:
        return split_body(queries, encoded, w_kv, retrieved)
    return plain_body(queries, encoded, w_kv, retrieved)


def solution(mesh):
    in_specs = (P("seq", "mp"), P("seq", None, None), P(None, None, "mp"), P("seq", None))
    out_specs = P("seq", "mp")
    return jax.shard_map(body, mesh=mesh, in_specs=in_specs, out_specs=out_specs, check_vma=False)
```

```python
import functools

import jax
import jax.numpy as jnp
from jax import lax
from jax.experimental import pallas as pl
from jax.experimental.pallas import tpu as pltpu
from jax.sharding import PartitionSpec as P

GROUP = 64
HEAD_DIM = 128
MIB = 1024 * 1024
PACE = 2 * 10**9
LIGHT = pl.CostEstimate(flops=1, bytes_accessed=1, transcendentals=0)


def in_vmem(value):
    return pltpu.with_memory_space_constraint(value, pltpu.VMEM)


def plan_kernel(capacity, ids_ref, stored_ref, slots_ref, own_ref, table_ref):
    seq_at, core = lax.axis_index("seq"), lax.rem(lax.axis_index("mp"), 2)
    tile_count = stored_ref.shape[0]
    bits = tile_count.bit_length() - 1
    half = capacity // 2
    counts = jnp.int32(0)
    for k in range(ids_ref.shape[0]):
        for c in range(ids_ref.shape[1]):
            tile_id = ids_ref[k, c]
            owner = lax.shift_right_logical(tile_id, bits)
            shift = owner * 4
            rank = lax.shift_right_logical(counts, shift) & (capacity - 1)
            counts += jnp.int32(1) << shift
            apart = owner ^ seq_at
            table_ref[apart * capacity + rank] = tile_id & (tile_count - 1)
            near = ((apart & 1) * capacity) + (rank ^ ((apart & 1) * core * half))
            far = ((apart & -2) + ((apart & 1) ^ core)) * capacity + rank
            slots_ref[2 * c + k] = jnp.where(apart < 2, near, far)
    for j in range(capacity):
        own_ref[j] = stored_ref[table_ref[j]]


def plan(ids, stored, capacity):
    smem, vmem = pl.BlockSpec(memory_space=pltpu.SMEM), pl.BlockSpec(memory_space=pltpu.VMEM)
    return pl.pallas_call(
        functools.partial(plan_kernel, capacity),
        out_shape=[
            jax.ShapeDtypeStruct((ids.size,), jnp.int32),
            pltpu.VMEM((capacity, *stored.shape[1:]), stored.dtype),
        ],
        in_specs=[smem, vmem],
        out_specs=[smem, vmem],
        scratch_shapes=[pltpu.SMEM((ids.size,), jnp.int32)],
        compiler_params=pltpu.CompilerParams(vmem_limit_bytes=16 * MIB),
        cost_estimate=LIGHT,
        name="plan",
    )(ids, stored)


def pick_kernel(plans, fetched, *refs):
    count = len(plans)
    asked, stored_ref, pieces = refs[:count], refs[count], refs[count + 1 : -5]
    here_ref, ids_at, table_ref, ids_sem, sem = refs[-5:]
    if fetched:
        here_ref, pieces = stored_ref, refs[count + 1 : -4]
    tile_count, rows, _ = stored_ref.shape
    fetches = [pltpu.make_async_copy(ref, ids_at.at[i], ids_sem.at[i]) for i, ref in enumerate(asked)]
    for fetch in fetches:
        fetch.start()
    load = None if fetched else pltpu.make_async_copy(stored_ref, here_ref, sem)
    if load is not None:
        load.start()
    lowest, mp_at = lax.axis_index("seq") * tile_count, lax.axis_index("mp")
    half = pl.multiple_of(mp_at // 2 * (rows // 2), rows // 2)
    for i in range(count):
        fetches[i].wait()
        found = jnp.int32(0)
        for k in range(ids_at.shape[1]):
            for c in range(ids_at.shape[2]):
                local = ids_at[i, k, c] - lowest
                table_ref[i, found] = local
                found += ((local >= 0) & (local < tile_count)).astype(jnp.int32)
    if load is not None:
        load.wait()
    at = 0
    for i, (kind, sizes) in enumerate(plans):
        rank = (mp_at % 2) * sizes[0] if kind == "tiles" else 0
        for size in sizes:
            for j in range(size):
                local = jnp.clip(table_ref[i, rank + j], 0, tile_count - 1)
                pieces[at][j] = here_ref[local, pl.ds(half, rows // 2), :] if kind == "rows" else here_ref[local]
            rank += size
            at += 1


def pick(asked, stored, plans, fetched):
    _, rows, width = stored.shape
    vmem = pl.BlockSpec(memory_space=pltpu.VMEM)
    shapes = [(size, rows // 2 if kind == "rows" else rows, width) for kind, sizes in plans for size in sizes]
    if not fetched:
        shapes.append(stored.shape)
    return pl.pallas_call(
        functools.partial(pick_kernel, plans, fetched),
        out_shape=[pltpu.VMEM(shape, stored.dtype) for shape in shapes],
        in_specs=[vmem] * len(asked) + [vmem if fetched else pl.BlockSpec(memory_space=pl.ANY)],
        out_specs=[vmem] * len(shapes),
        scratch_shapes=[
            pltpu.SMEM((len(plans), *asked[0].shape), jnp.int32),
            pltpu.SMEM((len(plans), asked[0].size + 1), jnp.int32),
            pltpu.SemaphoreType.DMA((len(plans),)),
            pltpu.SemaphoreType.DMA,
        ],
        compiler_params=pltpu.CompilerParams(vmem_limit_bytes=(16 if fetched else 52) * MIB),
        cost_estimate=LIGHT,
        name="pick",
    )(*[in_vmem(a) for a in asked], stored)


def turn_kernel(*refs):
    pass


def turn(values, others, flops):
    vmem = pl.BlockSpec(memory_space=pltpu.VMEM)
    count = len(values)
    return pl.pallas_call(
        turn_kernel,
        out_shape=[pltpu.VMEM(v.shape, v.dtype) for v in values],
        in_specs=[vmem] * count + [pl.BlockSpec(memory_space=pl.ANY)] * len(others),
        out_specs=[vmem] * count,
        input_output_aliases={i: i for i in range(count)},
        compiler_params=pltpu.CompilerParams(vmem_limit_bytes=16 * MIB),
        cost_estimate=pl.CostEstimate(flops=flops, bytes_accessed=1, transcendentals=0),
        name="turn",
    )(*[in_vmem(v) for v in values], *others)


def project_kernel(places, *refs):
    pieces, weights_ref, out_ref = refs[: len(places)], refs[len(places)], refs[-1]
    flat = jnp.concatenate([piece[...].reshape(-1, piece.shape[2]) for piece in pieces], axis=0)
    step = min(512, weights_ref.shape[1])
    for at in range(0, weights_ref.shape[1], step):
        columns = pl.ds(at, step)
        made = jnp.dot(flat, weights_ref[:, columns], preferred_element_type=jnp.float32).astype(jnp.bfloat16)
        done = 0
        for (tile, row), piece in zip(places, pieces):
            tiles, rows, _ = piece.shape
            part = made[done : done + tiles * rows].reshape(tiles, rows, -1)
            out_ref[pl.ds(tile, tiles), pl.ds(row, rows), columns] = part
            done += tiles * rows


def project(pieces, weights, held, shape, weight):
    count = len(pieces)
    vmem = pl.BlockSpec(memory_space=pltpu.VMEM)
    operands = [in_vmem(p) for _, _, p in pieces] + [weights]
    aliases = {}
    if held is not None:
        operands.append(held)
        aliases = {count + 1: 0}
    many = sum(p.shape[0] * p.shape[1] for _, _, p in pieces)
    return pl.pallas_call(
        functools.partial(project_kernel, [(tile, row) for tile, row, _ in pieces]),
        out_shape=pltpu.VMEM(shape, jnp.bfloat16),
        in_specs=[vmem] * len(operands),
        out_specs=vmem,
        input_output_aliases=aliases,
        compiler_params=pltpu.CompilerParams(vmem_limit_bytes=16 * MIB),
        cost_estimate=pl.CostEstimate(flops=many * weights.size * weight // 4, bytes_accessed=0, transcendentals=0),
        name="project",
    )(*operands)


def scores_of(queries, keys):
    both = lax.dot_general(
        jnp.concatenate(keys, axis=0),
        jnp.concatenate(queries, axis=0),
        (((1,), (1,)), ((), ())),
        preferred_element_type=jnp.float32,
    )
    rows = both.shape[0] // 2
    left = lax.broadcasted_iota(jnp.int32, (rows, both.shape[1]), 1) < both.shape[1] // 2
    return jnp.where(left, both[:rows], both[rows:])


def probs_of(scores):
    expd = jnp.exp((scores - jnp.max(scores, axis=0, keepdims=True)) * HEAD_DIM ** (-0.5))
    return (expd * (1.0 / jnp.sum(expd, axis=0, keepdims=True))).astype(jnp.bfloat16)


def mix(probs, values):
    both = lax.dot_general(
        probs, jnp.concatenate(values, axis=1), (((0,), (0,)), ((), ())), preferred_element_type=jnp.float32
    )
    half = both.shape[0] // 2
    return both[:half, :HEAD_DIM], both[half:, HEAD_DIM:]


def attend_kernel(heads, per, slots_ref, queries_ref, held_ref, out_ref, made_ref, sem):
    apart = 6
    groups = queries_ref.shape[0] // GROUP
    items = [(g, h) for g in range(groups) for h in range(0, heads, 2)]

    def part_of(g, h):
        one, two = slots_ref[2 * g], slots_ref[2 * g + 1]
        at = pl.ds(h * HEAD_DIM, HEAD_DIM)
        return jnp.concatenate([held_ref[one, :, at], held_ref[two, :, at]], axis=0)

    scores, probs, copies = {}, {}, []
    for now in range(len(items) + 2 * apart):
        if now < len(items):
            g, h = items[now]
            queries = [queries_ref[pl.ds(g * GROUP, GROUP), pl.ds((h + i) * HEAD_DIM, HEAD_DIM)] for i in range(2)]
            scores[now] = scores_of(queries, [part_of(g, h + i) for i in range(2)])
        if apart <= now < len(items) + apart:
            probs[now - apart] = probs_of(scores.pop(now - apart))
        if 2 * apart <= now:
            g, h = items[now - 2 * apart]
            mixed = mix(probs.pop(now - 2 * apart), [part_of(g, heads + h + i) for i in range(2)])
            for i in range(2):
                made_ref[pl.ds(g * GROUP, GROUP), pl.ds((h + i) * HEAD_DIM, HEAD_DIM)] = mixed[i].astype(jnp.bfloat16)
            if h == heads - 2 and g % per == per - 1:
                done = pl.ds((g + 1 - per) * GROUP, per * GROUP)
                copies.append(pltpu.make_async_copy(made_ref.at[done], out_ref.at[done], sem.at[g // per]))
                copies[-1].start()
    for copy in copies:
        copy.wait()


def attend(queries, held, slots, heads):
    groups = queries.shape[0] // GROUP
    per = 2 if groups % 2 == 0 else 1
    vmem = pl.BlockSpec(memory_space=pltpu.VMEM)
    return pl.pallas_call(
        functools.partial(attend_kernel, heads, per),
        out_shape=jax.ShapeDtypeStruct(queries.shape, jnp.bfloat16),
        in_specs=[pl.BlockSpec(memory_space=pltpu.SMEM), vmem, vmem],
        out_specs=pl.BlockSpec(memory_space=pl.ANY),
        scratch_shapes=[pltpu.VMEM(queries.shape, jnp.bfloat16), pltpu.SemaphoreType.DMA((groups // per,))],
        compiler_params=pltpu.CompilerParams(vmem_limit_bytes=24 * MIB),
        cost_estimate=pl.CostEstimate(flops=10**9, bytes_accessed=16 * MIB, transcendentals=10**6),
        name="attend",
    )(slots, in_vmem(queries), in_vmem(held))


def ref_ranks(owners):
    length = owners.shape[-1]
    position = jnp.arange(length)
    earlier = position[None, :] < position[:, None]
    same_owner = owners[..., :, None] == owners[..., None, :]
    return jnp.sum(same_owner & earlier, axis=-1)


def plain_body(queries, encoded, w_kv, retrieved):
    seq_count = lax.axis_size("seq")
    ref_count = 2 * retrieved.shape[0]
    tile_count = encoded.shape[0]
    capacity = (ref_count + seq_count - 1) // seq_count
    tile_ids = retrieved.reshape(ref_count)
    owners = tile_ids // tile_count
    slot_ids = owners * capacity + ref_ranks(owners)
    wanted = jnp.arange(seq_count * capacity, dtype=jnp.int32)[:, None] == slot_ids[None, :]
    request = jnp.sum(jnp.where(wanted, (tile_ids % tile_count)[None, :], 0), axis=1)
    asked = lax.all_to_all(request, "seq", split_axis=0, concat_axis=0, tiled=True)
    outgoing = jnp.take(encoded, asked, axis=0, mode="clip")
    tiles = lax.all_to_all(outgoing, "seq", split_axis=0, concat_axis=0, tiled=True)
    weights = w_kv.reshape(w_kv.shape[0], -1)
    flat = jnp.dot(tiles.reshape(-1, tiles.shape[2]), weights, preferred_element_type=jnp.float32)
    held = flat.astype(jnp.bfloat16).reshape(tiles.shape[0], tiles.shape[1], -1)
    return attend(queries, held, slot_ids, queries.shape[1] // HEAD_DIM)


def split_body(queries, encoded, w_kv, retrieved):
    seq_count, mp_count = lax.axis_size("seq"), lax.axis_size("mp")
    ref_count = 2 * retrieved.shape[0]
    tile_count, rows, width = encoded.shape
    capacity = ref_count // seq_count
    both = ("seq", "mp")

    def joint(move):
        return [(s * mp_count + m, move(s, m)) for s in range(seq_count) for m in range(mp_count)]

    def across(value, part):
        if part == 0:
            return lax.ppermute(value, "seq", [(s, s ^ 1) for s in range(seq_count)])
        return lax.ppermute(value, both, joint(lambda s, m: (s ^ (2 * part) ^ (m % 2)) * mp_count + m))

    def over_mp(value, flip):
        return lax.ppermute(value, "mp", [(m, m ^ flip) for m in range(mp_count)])


    ids = retrieved.T
    size, early = capacity // 2, capacity // 2

    def spread(mine, first):
        theirs = over_mp(mine, 2)
        return [
            (first, 0, mine),
            (first, rows // 2, theirs),
            (first + capacity, 0, over_mp(mine, 1)),
            (first + capacity, rows // 2, over_mp(theirs, 1)),
        ]

    asked = {p: across(ids, p) for p in (2, 3, 1, 0)}
    kinds = [("rows", [capacity])]
    picked2, stored = pick([asked[p] for p in (2,)], encoded, kinds, False)
    kinds = [("rows", [capacity]), ("all", [early, capacity - early]), ("tiles", [size])]
    picked3, *picked1, beside = pick([asked[p] for p in (3, 1, 0)], stored, kinds, True)
    picked2 = turn([picked2], [asked[p] for p in (3, 1, 0)], 1)[0]
    got2, got1, beside = across(picked2, 2), across(picked1[0], 1), across(beside, 0)
    weights = in_vmem(w_kv.reshape(width, -1))
    slots, own = plan(ids, stored, capacity)
    shape = (ref_count, rows, weights.shape[1])

    def add(held, pieces, weight):
        return project(pieces, weights, held, shape, weight)

    def core(value, tile, row, cuts):
        step = value.shape[0] // cuts
        return [(tile + at, row, over_mp(value[at : at + step], 1)) for at in range(0, value.shape[0], step)]

    at1, at2, at3 = 2 * capacity, 4 * capacity, 6 * capacity
    held = add(None, [(0, 0, own)], 1)
    picked3 = turn([picked3], [got2, held, slots], PACE)[0]
    next1, beside, got1, got2 = turn([picked1[1], beside, got1, got2], [picked3], 1)
    got3, rest1, theirs2 = across(picked3, 3), across(next1, 1), over_mp(got2, 2)
    held = add(held, [(capacity, 0, beside), *core(beside, capacity + size, 0, 2)], 1)
    held = add(held, [(at2, 0, got2), *core(got2, at2 + capacity, 0, 2)], 1)
    held = add(held, [(at1, 0, got1), *core(got1, at1 + capacity, 0, 1 if early % 2 else 2)], 1)
    got3 = turn([got3], [held], PACE)[0]
    theirs3 = over_mp(got3, 2)
    queries = in_vmem(queries)
    theirs2 = turn([theirs2], [got3], 1)[0]
    rest1 = turn([rest1], [theirs2, queries], 1)[0]
    held = add(held, [(at2, rows // 2, theirs2), *core(theirs2, at2 + capacity, rows // 2, 2)], 1)
    held = add(held, [(at1 + early, 0, rest1), *core(rest1, at1 + capacity + early, 0, 1 if early % 2 or early > size else 2)], 1)
    theirs3 = turn([theirs3], [held], 1)[0]
    held = add(held, [(at3, 0, got3), *core(got3, at3 + capacity, 0, 1)], 64)
    held = add(held, [(at3, rows // 2, theirs3), *core(theirs3, at3 + capacity, rows // 2, 1)], 64)
    return attend(queries, held, slots, queries.shape[1] // HEAD_DIM)


def body(queries, encoded, w_kv, retrieved):
    seq_count, mp_count = lax.axis_size("seq"), lax.axis_size("mp")
    ref_count = 2 * retrieved.shape[0]
    few = seq_count == 8 and mp_count == 4
    capacity, tile_count = ref_count // seq_count, encoded.shape[0]
    even = capacity * seq_count == ref_count and capacity == 8 and tile_count & (tile_count - 1) == 0
    if few and even and encoded.shape[1] % 32 == 0:
        return split_body(queries, encoded, w_kv, retrieved)
    return plain_body(queries, encoded, w_kv, retrieved)


def solution(mesh):
    in_specs = (P("seq", "mp"), P("seq", None, None), P(None, None, "mp"), P("seq", None))
    out_specs = P("seq", "mp")
    return jax.shard_map(body, mesh=mesh, in_specs=in_specs, out_specs=out_specs, check_vma=False)
```

```python
import functools

import jax
import jax.numpy as jnp
from jax import lax
from jax.experimental import pallas as pl
from jax.experimental.pallas import tpu as pltpu
from jax.sharding import PartitionSpec as P

GROUP = 64
HEAD_DIM = 128
MIB = 1024 * 1024
PACE = 2 * 10**9
LIGHT = pl.CostEstimate(flops=1, bytes_accessed=1, transcendentals=0)


def in_vmem(value):
    return pltpu.with_memory_space_constraint(value, pltpu.VMEM)


def plan_kernel(capacity, ids_ref, stored_ref, slots_ref, own_ref, table_ref):
    seq_at, core = lax.axis_index("seq"), lax.rem(lax.axis_index("mp"), 2)
    tile_count = stored_ref.shape[0]
    bits = tile_count.bit_length() - 1
    half = capacity // 2
    counts = jnp.int32(0)
    for k in range(ids_ref.shape[0]):
        for c in range(ids_ref.shape[1]):
            tile_id = ids_ref[k, c]
            owner = lax.shift_right_logical(tile_id, bits)
            shift = owner * 4
            rank = lax.shift_right_logical(counts, shift) & (capacity - 1)
            counts += jnp.int32(1) << shift
            apart = owner ^ seq_at
            table_ref[apart * capacity + rank] = tile_id & (tile_count - 1)
            near = ((apart & 1) * capacity) + (rank ^ ((apart & 1) * core * half))
            far = ((apart & -2) + ((apart & 1) ^ core)) * capacity + rank
            slots_ref[2 * c + k] = jnp.where(apart < 2, near, far)
    for j in range(capacity):
        own_ref[j] = stored_ref[table_ref[j]]


def plan(ids, stored, capacity):
    smem, vmem = pl.BlockSpec(memory_space=pltpu.SMEM), pl.BlockSpec(memory_space=pltpu.VMEM)
    return pl.pallas_call(
        functools.partial(plan_kernel, capacity),
        out_shape=[
            jax.ShapeDtypeStruct((ids.size,), jnp.int32),
            pltpu.VMEM((capacity, *stored.shape[1:]), stored.dtype),
        ],
        in_specs=[smem, vmem],
        out_specs=[smem, vmem],
        scratch_shapes=[pltpu.SMEM((ids.size,), jnp.int32)],
        compiler_params=pltpu.CompilerParams(vmem_limit_bytes=16 * MIB),
        cost_estimate=LIGHT,
        name="plan",
    )(ids, stored)


def pick_kernel(plans, fetched, *refs):
    count = len(plans)
    asked, stored_ref, pieces = refs[:count], refs[count], refs[count + 1 : -5]
    here_ref, ids_at, table_ref, ids_sem, sem = refs[-5:]
    if fetched:
        here_ref, pieces = stored_ref, refs[count + 1 : -4]
    tile_count, rows, _ = stored_ref.shape
    fetches = [pltpu.make_async_copy(ref, ids_at.at[i], ids_sem.at[i]) for i, ref in enumerate(asked)]
    for fetch in fetches:
        fetch.start()
    load = None if fetched else pltpu.make_async_copy(stored_ref, here_ref, sem)
    if load is not None:
        load.start()
    lowest, mp_at = lax.axis_index("seq") * tile_count, lax.axis_index("mp")
    half = pl.multiple_of(mp_at // 2 * (rows // 2), rows // 2)
    for i in range(count):
        fetches[i].wait()
        found = jnp.int32(0)
        for k in range(ids_at.shape[1]):
            for c in range(ids_at.shape[2]):
                local = ids_at[i, k, c] - lowest
                table_ref[i, found] = local
                found += ((local >= 0) & (local < tile_count)).astype(jnp.int32)
    if load is not None:
        load.wait()
    at = 0
    for i, (kind, sizes) in enumerate(plans):
        rank = (mp_at % 2) * sizes[0] if kind == "tiles" else 0
        for size in sizes:
            for j in range(size):
                local = jnp.clip(table_ref[i, rank + j], 0, tile_count - 1)
                pieces[at][j] = here_ref[local, pl.ds(half, rows // 2), :] if kind == "rows" else here_ref[local]
            rank += size
            at += 1


def pick(asked, stored, plans, fetched):
    _, rows, width = stored.shape
    vmem = pl.BlockSpec(memory_space=pltpu.VMEM)
    shapes = [(size, rows // 2 if kind == "rows" else rows, width) for kind, sizes in plans for size in sizes]
    if not fetched:
        shapes.append(stored.shape)
    return pl.pallas_call(
        functools.partial(pick_kernel, plans, fetched),
        out_shape=[pltpu.VMEM(shape, stored.dtype) for shape in shapes],
        in_specs=[vmem] * len(asked) + [vmem if fetched else pl.BlockSpec(memory_space=pl.ANY)],
        out_specs=[vmem] * len(shapes),
        scratch_shapes=[
            pltpu.SMEM((len(plans), *asked[0].shape), jnp.int32),
            pltpu.SMEM((len(plans), asked[0].size + 1), jnp.int32),
            pltpu.SemaphoreType.DMA((len(plans),)),
            pltpu.SemaphoreType.DMA,
        ],
        compiler_params=pltpu.CompilerParams(vmem_limit_bytes=(16 if fetched else 52) * MIB),
        cost_estimate=LIGHT,
        name="pick",
    )(*[in_vmem(a) for a in asked], stored)


def turn_kernel(*refs):
    pass


def turn(values, others, flops):
    vmem = pl.BlockSpec(memory_space=pltpu.VMEM)
    count = len(values)
    return pl.pallas_call(
        turn_kernel,
        out_shape=[pltpu.VMEM(v.shape, v.dtype) for v in values],
        in_specs=[vmem] * count + [pl.BlockSpec(memory_space=pl.ANY)] * len(others),
        out_specs=[vmem] * count,
        input_output_aliases={i: i for i in range(count)},
        compiler_params=pltpu.CompilerParams(vmem_limit_bytes=16 * MIB),
        cost_estimate=pl.CostEstimate(flops=flops, bytes_accessed=1, transcendentals=0),
        name="turn",
    )(*[in_vmem(v) for v in values], *others)


def project_kernel(places, *refs):
    pieces, weights_ref, out_ref = refs[: len(places)], refs[len(places)], refs[-1]
    flat = jnp.concatenate([piece[...].reshape(-1, piece.shape[2]) for piece in pieces], axis=0)
    step = min(2048, weights_ref.shape[1])
    for at in range(0, weights_ref.shape[1], step):
        columns = pl.ds(at, step)
        made = jnp.dot(flat, weights_ref[:, columns], preferred_element_type=jnp.float32).astype(jnp.bfloat16)
        done = 0
        for (tile, row), piece in zip(places, pieces):
            tiles, rows, _ = piece.shape
            part = made[done : done + tiles * rows].reshape(tiles, rows, -1)
            out_ref[pl.ds(tile, tiles), pl.ds(row, rows), columns] = part
            done += tiles * rows


def project(pieces, weights, held, shape, weight):
    count = len(pieces)
    vmem = pl.BlockSpec(memory_space=pltpu.VMEM)
    operands = [in_vmem(p) for _, _, p in pieces] + [weights]
    aliases = {}
    if held is not None:
        operands.append(held)
        aliases = {count + 1: 0}
    many = sum(p.shape[0] * p.shape[1] for _, _, p in pieces)
    return pl.pallas_call(
        functools.partial(project_kernel, [(tile, row) for tile, row, _ in pieces]),
        out_shape=pltpu.VMEM(shape, jnp.bfloat16),
        in_specs=[vmem] * len(operands),
        out_specs=vmem,
        input_output_aliases=aliases,
        compiler_params=pltpu.CompilerParams(vmem_limit_bytes=16 * MIB),
        cost_estimate=pl.CostEstimate(flops=many * weights.size * weight // 4, bytes_accessed=0, transcendentals=0),
        name="project",
    )(*operands)


def scores_of(queries, keys):
    both = lax.dot_general(
        jnp.concatenate(keys, axis=0),
        jnp.concatenate(queries, axis=0),
        (((1,), (1,)), ((), ())),
        preferred_element_type=jnp.float32,
    )
    rows = both.shape[0] // 2
    left = lax.broadcasted_iota(jnp.int32, (rows, both.shape[1]), 1) < both.shape[1] // 2
    return jnp.where(left, both[:rows], both[rows:])


def probs_of(scores):
    expd = jnp.exp((scores - jnp.max(scores, axis=0, keepdims=True)) * HEAD_DIM ** (-0.5))
    return (expd * (1.0 / jnp.sum(expd, axis=0, keepdims=True))).astype(jnp.bfloat16)


def mix(probs, values):
    both = lax.dot_general(
        probs, jnp.concatenate(values, axis=1), (((0,), (0,)), ((), ())), preferred_element_type=jnp.float32
    )
    half = both.shape[0] // 2
    return both[:half, :HEAD_DIM], both[half:, HEAD_DIM:]


def attend_kernel(heads, per, slots_ref, queries_ref, held_ref, out_ref, made_ref, sem):
    apart = 6
    groups = queries_ref.shape[0] // GROUP
    items = [(g, h) for g in range(groups) for h in range(0, heads, 2)]

    def part_of(g, h):
        one, two = slots_ref[2 * g], slots_ref[2 * g + 1]
        at = pl.ds(h * HEAD_DIM, HEAD_DIM)
        return jnp.concatenate([held_ref[one, :, at], held_ref[two, :, at]], axis=0)

    scores, probs, copies = {}, {}, []
    for now in range(len(items) + 2 * apart):
        if now < len(items):
            g, h = items[now]
            queries = [queries_ref[pl.ds(g * GROUP, GROUP), pl.ds((h + i) * HEAD_DIM, HEAD_DIM)] for i in range(2)]
            scores[now] = scores_of(queries, [part_of(g, h + i) for i in range(2)])
        if apart <= now < len(items) + apart:
            probs[now - apart] = probs_of(scores.pop(now - apart))
        if 2 * apart <= now:
            g, h = items[now - 2 * apart]
            mixed = mix(probs.pop(now - 2 * apart), [part_of(g, heads + h + i) for i in range(2)])
            for i in range(2):
                made_ref[pl.ds(g * GROUP, GROUP), pl.ds((h + i) * HEAD_DIM, HEAD_DIM)] = mixed[i].astype(jnp.bfloat16)
            if h == heads - 2 and g % per == per - 1:
                done = pl.ds((g + 1 - per) * GROUP, per * GROUP)
                copies.append(pltpu.make_async_copy(made_ref.at[done], out_ref.at[done], sem.at[g // per]))
                copies[-1].start()
    for copy in copies:
        copy.wait()


def attend(queries, held, slots, heads):
    groups = queries.shape[0] // GROUP
    per = 2 if groups % 2 == 0 else 1
    vmem = pl.BlockSpec(memory_space=pltpu.VMEM)
    return pl.pallas_call(
        functools.partial(attend_kernel, heads, per),
        out_shape=jax.ShapeDtypeStruct(queries.shape, jnp.bfloat16),
        in_specs=[pl.BlockSpec(memory_space=pltpu.SMEM), vmem, vmem],
        out_specs=pl.BlockSpec(memory_space=pl.ANY),
        scratch_shapes=[pltpu.VMEM(queries.shape, jnp.bfloat16), pltpu.SemaphoreType.DMA((groups // per,))],
        compiler_params=pltpu.CompilerParams(vmem_limit_bytes=24 * MIB),
        cost_estimate=pl.CostEstimate(flops=10**9, bytes_accessed=16 * MIB, transcendentals=10**6),
        name="attend",
    )(slots, in_vmem(queries), in_vmem(held))


def ref_ranks(owners):
    length = owners.shape[-1]
    position = jnp.arange(length)
    earlier = position[None, :] < position[:, None]
    same_owner = owners[..., :, None] == owners[..., None, :]
    return jnp.sum(same_owner & earlier, axis=-1)


def plain_body(queries, encoded, w_kv, retrieved):
    seq_count = lax.axis_size("seq")
    ref_count = 2 * retrieved.shape[0]
    tile_count = encoded.shape[0]
    capacity = (ref_count + seq_count - 1) // seq_count
    tile_ids = retrieved.reshape(ref_count)
    owners = tile_ids // tile_count
    slot_ids = owners * capacity + ref_ranks(owners)
    wanted = jnp.arange(seq_count * capacity, dtype=jnp.int32)[:, None] == slot_ids[None, :]
    request = jnp.sum(jnp.where(wanted, (tile_ids % tile_count)[None, :], 0), axis=1)
    asked = lax.all_to_all(request, "seq", split_axis=0, concat_axis=0, tiled=True)
    outgoing = jnp.take(encoded, asked, axis=0, mode="clip")
    tiles = lax.all_to_all(outgoing, "seq", split_axis=0, concat_axis=0, tiled=True)
    weights = w_kv.reshape(w_kv.shape[0], -1)
    flat = jnp.dot(tiles.reshape(-1, tiles.shape[2]), weights, preferred_element_type=jnp.float32)
    held = flat.astype(jnp.bfloat16).reshape(tiles.shape[0], tiles.shape[1], -1)
    return attend(queries, held, slot_ids, queries.shape[1] // HEAD_DIM)


def split_body(queries, encoded, w_kv, retrieved):
    seq_count, mp_count = lax.axis_size("seq"), lax.axis_size("mp")
    ref_count = 2 * retrieved.shape[0]
    tile_count, rows, width = encoded.shape
    capacity = ref_count // seq_count
    both = ("seq", "mp")

    def joint(move):
        return [(s * mp_count + m, move(s, m)) for s in range(seq_count) for m in range(mp_count)]

    def across(value, part):
        if part == 0:
            return lax.ppermute(value, "seq", [(s, s ^ 1) for s in range(seq_count)])
        return lax.ppermute(value, both, joint(lambda s, m: (s ^ (2 * part) ^ (m % 2)) * mp_count + m))

    def over_mp(value, flip):
        return lax.ppermute(value, "mp", [(m, m ^ flip) for m in range(mp_count)])


    ids = retrieved.T
    size, early = capacity // 2, capacity // 2

    def spread(mine, first):
        theirs = over_mp(mine, 2)
        return [
            (first, 0, mine),
            (first, rows // 2, theirs),
            (first + capacity, 0, over_mp(mine, 1)),
            (first + capacity, rows // 2, over_mp(theirs, 1)),
        ]

    asked = {p: across(ids, p) for p in (2, 3, 1, 0)}
    kinds = [("rows", [capacity])]
    picked2, stored = pick([asked[p] for p in (2,)], encoded, kinds, False)
    kinds = [("rows", [capacity]), ("all", [early, capacity - early]), ("tiles", [size])]
    picked3, *picked1, beside = pick([asked[p] for p in (3, 1, 0)], stored, kinds, True)
    picked2 = turn([picked2], [asked[p] for p in (3, 1, 0)], 1)[0]
    got2, got1, beside = across(picked2, 2), across(picked1[0], 1), across(beside, 0)
    weights = in_vmem(w_kv.reshape(width, -1))
    slots, own = plan(ids, stored, capacity)
    shape = (ref_count, rows, weights.shape[1])

    def add(held, pieces, weight):
        return project(pieces, weights, held, shape, weight)

    def core(value, tile, row, cuts):
        step = value.shape[0] // cuts
        return [(tile + at, row, over_mp(value[at : at + step], 1)) for at in range(0, value.shape[0], step)]

    at1, at2, at3 = 2 * capacity, 4 * capacity, 6 * capacity
    held = add(None, [(0, 0, own)], 1)
    picked3 = turn([picked3], [got2, held, slots], PACE)[0]
    next1, beside, got1, got2 = turn([picked1[1], beside, got1, got2], [picked3], 1)
    got3, rest1, theirs2 = across(picked3, 3), across(next1, 1), over_mp(got2, 2)
    held = add(held, [(capacity, 0, beside), *core(beside, capacity + size, 0, 2)], 1)
    held = add(held, [(at2, 0, got2), *core(got2, at2 + capacity, 0, 2)], 1)
    held = add(held, [(at1, 0, got1), *core(got1, at1 + capacity, 0, 1 if early % 2 else 2)], 1)
    got3 = turn([got3], [held], PACE)[0]
    theirs3 = over_mp(got3, 2)
    queries = in_vmem(queries)
    theirs2 = turn([theirs2], [got3], 1)[0]
    rest1 = turn([rest1], [theirs2, queries], 1)[0]
    held = add(held, [(at2, rows // 2, theirs2), *core(theirs2, at2 + capacity, rows // 2, 2)], 1)
    held = add(held, [(at1 + early, 0, rest1), *core(rest1, at1 + capacity + early, 0, 1 if early % 2 or early > size else 2)], 1)
    theirs3 = turn([theirs3], [held], 1)[0]
    held = add(held, [(at3, 0, got3), *core(got3, at3 + capacity, 0, 1)], 64)
    held = add(held, [(at3, rows // 2, theirs3), *core(theirs3, at3 + capacity, rows // 2, 1)], 64)
    return attend(queries, held, slots, queries.shape[1] // HEAD_DIM)


def body(queries, encoded, w_kv, retrieved):
    seq_count, mp_count = lax.axis_size("seq"), lax.axis_size("mp")
    ref_count = 2 * retrieved.shape[0]
    few = seq_count == 8 and mp_count == 4
    capacity, tile_count = ref_count // seq_count, encoded.shape[0]
    even = capacity * seq_count == ref_count and capacity == 8 and tile_count & (tile_count - 1) == 0
    if few and even and encoded.shape[1] % 32 == 0:
        return split_body(queries, encoded, w_kv, retrieved)
    return plain_body(queries, encoded, w_kv, retrieved)


def solution(mesh):
    in_specs = (P("seq", "mp"), P("seq", None, None), P(None, None, "mp"), P("seq", None))
    out_specs = P("seq", "mp")
    return jax.shard_map(body, mesh=mesh, in_specs=in_specs, out_specs=out_specs, check_vma=False)
```
